32 devices in a mesh: tok: 8 (over z, x), hid: 4 (over y, core).
Axes of the slice: x: 2, y: 2, z: 4, core: 2. Of those that a mesh axis runs over, the one named last changes fastest.
Arguments:
- inputs: float32 [1024, 4096], P('tok'), may hold values from -6 to 6
- cotangent: float32 [1024, 4096], P('tok'), may hold values from -6 to 6
- up_blocks: float32 [112, 4, 128, 128], P('hid', None, 'tok'), may hold values from -0.25 to 0.25
- down_blocks: float32 [112, 4, 128, 128], P('hid', None, 'tok'), may hold values from -0.25 to 0.25
- up_index: int32 [112, 4], P('hid'), may hold values from 0 to 31, all different within a row
- down_index: int32 [112, 4], P('hid'), may hold values from 0 to 31, all different within a row
- mom_up: float32 [112, 4, 128, 128], P('hid', None, 'tok'), may hold values from -6 to 6
- mom_down: float32 [112, 4, 128, 128], P('hid', None, 'tok'), may hold values from -6 to 6
Outputs:
- input_grad: float32 [1024, 4096], P('tok', 'hid')
- new_mom_up: float32 [112, 4, 128, 128], P('hid', None, 'tok')
- new_mom_down: float32 [112, 4, 128, 128], P('hid', None, 'tok')
The draws below stay inside these ranges and needn't reach their ends.
Inputs may be any that keep to these rules, and one draw needn't show every extreme that they name: `up_index`: each row lists 4 different model blocks, and every model block appears in some row. `down_index`: each row lists 4 different model blocks, and every model block appears in some row.
All inputs are finite; a program needn't handle non-finite values.
Results may differ from the reference program's by a relative error of at most 0.0003.
Values sent between devices are 32-bit elements; how exact they have to be, the bound alone decides.
No kernel may reach another device: no remote copies, remote signals or barrier semaphores. Data moves between devices by JAX's collectives and lax.ppermute only.
A program may use at most 128 MiB of HBM per device.

```python
import jax
import jax.numpy as jnp
from jax import lax

D = 4096
BLK = 128
KB = 4
TOKENS = 1024
FFB = 112


def shard_levels(own_key, extent, pieces, low, largest):
    def one(position, parts):
        heights = jax.random.uniform(jax.random.fold_in(jax.random.fold_in(own_key, 6), position), (parts,), jnp.float32, low / len(pieces), largest / len(pieces))
        return jnp.repeat(jnp.exp(heights), extent[position] // parts).reshape((-1,) + (1,) * (len(extent) - position - 1))

    level = one(*pieces[0])
    for cut in pieces[1:]:
        level = level * one(*cut)
    return level


def picks_of(rng, rows, count, top, lift):
    ranking = jax.random.permutation(jax.random.fold_in(rng, 1), count)
    boost = ranking
    for power in range(3):
        boost = boost * boost // count
    boost = boost * lift // count
    chance = jax.random.randint(jax.random.fold_in(rng, 2), (rows, count), 0, 4096) + boost
    holders = jax.random.permutation(jax.random.fold_in(rng, 3), rows)[jnp.arange(count) % rows]
    chance = jnp.where(jnp.arange(rows)[:, None] == holders[None, :], 1 << 14, chance)
    score = chance * count + jnp.arange(count)
    return lax.top_k(score.astype(jnp.int32), top)[1].astype(jnp.int32)


def gaussian(own_key, extent, scale, reach, pieces=(), held_as=jnp.bfloat16):
    array = jax.random.normal(own_key, extent, jnp.float32) * scale
    if len(pieces) > 0:
        array = shard_levels(own_key, extent, pieces, -0.22, 0.18) * array
    return jnp.clip(array, min=-reach, max=reach).astype(held_as)


def setup_inputs(seed: int = 0) -> dict:
    streams_of = jax.random.split(jax.random.key(seed), 9)
    return {
        "inputs": gaussian(streams_of[0], (TOKENS, D), 1.0, 6.0, ((0, 8),), jnp.float32),
        "cotangent": gaussian(streams_of[1], (TOKENS, D), 1.0, 6.0, ((0, 8),), jnp.float32),
        "up_blocks": gaussian(streams_of[2], (FFB, KB, BLK, BLK), (KB * BLK) ** -0.5, 0.25, ((0, 4), (2, 8)), jnp.float32),
        "down_blocks": gaussian(streams_of[3], (FFB, KB, BLK, BLK), (KB * BLK) ** -0.5, 0.25, ((0, 4), (2, 8)), jnp.float32),
        "up_index": picks_of(streams_of[4], FFB, D // BLK, KB, 0),
        "down_index": picks_of(streams_of[5], FFB, D // BLK, KB, 0),
        "mom_up": gaussian(streams_of[6], (FFB, KB, BLK, BLK), 1.0, 6.0, ((0, 4), (2, 8)), jnp.float32),
        "mom_down": gaussian(streams_of[7], (FFB, KB, BLK, BLK), 1.0, 6.0, ((0, 4), (2, 8)), jnp.float32),
    }


def reference(inputs, cotangent, up_blocks, down_blocks, up_index, down_index, mom_up, mom_down):
    token_count = inputs.shape[0]
    block = up_blocks.shape[2]
    x_blocks = inputs.reshape(token_count, -1, block)
    cot_blocks = cotangent.reshape(token_count, -1, block)
    grad_scale = token_count ** -0.5
    highest = lax.Precision.HIGHEST

    def block_step(carried, scan_item):
        w_up, w_down, up_row, down_row = scan_item
        x_sel = jnp.take(x_blocks, up_row.astype(jnp.int32), axis=1)
        cot_sel = jnp.take(cot_blocks, down_row.astype(jnp.int32), axis=1)
        pre_act = jnp.einsum('tkd,kdc->tc', x_sel, w_up, precision=highest)
        sigmoid_pre = jax.nn.sigmoid(pre_act)
        activation = pre_act * sigmoid_pre
        grad_act = jnp.einsum('tkd,kcd->tc', cot_sel, w_down, precision=highest)
        grad_pre = grad_act * sigmoid_pre * (1.0 + pre_act * (1.0 - sigmoid_pre))
        back_terms = jnp.einsum('tc,kdc->tkd', grad_pre, w_up, precision=highest)
        carried = carried.at[:, up_row.astype(jnp.int32)].add(back_terms)
        grad_up = grad_scale * jnp.einsum('tkd,tc->kdc', x_sel, grad_pre, precision=highest)
        grad_down = grad_scale * jnp.einsum('tc,tkd->kcd', activation, cot_sel, precision=highest)
        return carried, (grad_up, grad_down)

    start_grad = jnp.zeros(x_blocks.shape, jnp.float32)
    input_grad, (grad_up, grad_down) = lax.scan(block_step, start_grad, (up_blocks, down_blocks, up_index, down_index))
    return input_grad.reshape(token_count, -1), 0.9 * mom_up + grad_up, 0.9 * mom_down + grad_down
```

```python
import functools

import jax
import jax.numpy as jnp
from jax import lax
from jax.experimental import pallas as pl
from jax.experimental.pallas import tpu as pltpu
from jax.sharding import PartitionSpec as P

F32, BF16 = jnp.float32, jnp.bfloat16
NN = (((1,), (0,)), ((), ()))
NT = (((1,), (1,)), ((), ()))


def swap(value, axis, bit):
    size = lax.axis_size(axis)
    return lax.ppermute(value, axis, [(i, i ^ bit) for i in range(size)])


def bits_below(size):
    return [1 << i for i in range(size.bit_length() - 1)]


def inner_size(size):
    inner = 1
    while inner * inner * 8 <= size:
        inner *= 2
    return inner


def split(value):
    high = value.astype(BF16)
    return high, (value - high.astype(F32)).astype(BF16)


def dot(a, b, dims):
    return lax.dot_general(a, b, dims, preferred_element_type=F32)


def kernel(cfg, up_at, down_at, place, *refs):
    fc, kb, blk, rows, nb, n, q, heads, first, last = cfg
    refs = list(refs)
    x_own, c_own, xc_got = refs[:3]
    slabs = refs[3:3 + n]
    refs = refs[3 + n:]
    prev = None
    if not first:
        prev, refs = refs[0], refs[1:]
    if n > 1:
        (g0, g1), refs = refs[:2], refs[2:]
    else:
        g0, refs = refs[0], refs[1:]
    if last:
        outs, refs = refs[:2], refs[2:]
    else:
        outs, refs = refs[:1], refs[1:]
    w, g, xb, cb, acc, w_sem, g_sem, x_sem, i_sem = refs
    me, hid = place[0], place[1]

    def weight_copy(r):
        start = pl.multiple_of((me ^ r) * q, q) if n > 1 else 0
        return pltpu.make_async_copy(slabs[r], w.at[:, :, :, pl.ds(start, q), :], w_sem.at[r])

    def grad_copy(r):
        start = pl.multiple_of((me ^ r) * q, q) if n > 1 else 0
        out = g0 if r % 2 == 0 else g1
        return pltpu.make_async_copy(g.at[:, :, :, pl.ds(start, q), :], out.at[r // 2], g_sem.at[r])

    def token_copies(f, slot):
        copies = []
        for k in range(kb):
            up_col = pl.multiple_of(up_at[f * kb + k] * blk, blk)
            down_col = pl.multiple_of(down_at[f * kb + k] * blk, blk)
            for i, (src, col, buf) in enumerate((
                (x_own, up_col, xb.at[slot, k, pl.ds(0, rows)]),
                (xc_got.at[0], up_col, xb.at[slot, k, pl.ds(rows, rows)]),
                (c_own, down_col, cb.at[slot, k, pl.ds(0, rows)]),
                (xc_got.at[1], down_col, cb.at[slot, k, pl.ds(rows, rows)]),
            )):
                copies.append(pltpu.make_async_copy(
                    src.at[:, pl.ds(col, blk)], buf, x_sem.at[slot, 4 * k + i]))
        return copies

    for r in range(n):
        weight_copy(r).start()
    for copy in token_copies(0, 0):
        copy.start()
    if first:
        acc[...] = jnp.zeros_like(acc)
    else:
        fill = pltpu.make_async_copy(prev, acc, i_sem.at[0])
        fill.start()
        fill.wait()
    for r in range(n):
        weight_copy(r).wait()

    def step(f, carry):
        slot = lax.rem(f, 2)

        @pl.when(f + 1 < fc)
        def _():
            for copy in token_copies(f + 1, 1 - slot):
                copy.start()

        for copy in token_copies(f, slot):
            copy.wait()
        xh, xl = split(jnp.concatenate([xb[slot, k] for k in range(kb)], axis=1))
        ch, cl = split(jnp.concatenate([cb[slot, k] for k in range(kb)], axis=1))
        uh, ul = split(w[0, f].reshape(kb * blk, blk))
        dh, dl = split(jnp.concatenate([w[1, f, k] for k in range(kb)], axis=1))

        wide = dot(xh, jnp.concatenate([uh, ul], axis=1), NN)
        pre = wide[:, :blk] + (wide[:, blk:] + dot(xl, uh, NN))
        wide = dot(ch, jnp.concatenate([dh, dl], axis=0), NT)
        grad_act = wide[:, :blk] + (wide[:, blk:] + dot(cl, dh, NT))
        sig = jax.nn.sigmoid(pre)
        act = pre * sig
        grad_pre = grad_act * sig * (1.0 + pre * (1.0 - sig))

        ah, al = split(act.T)
        tall = dot(jnp.concatenate([ah, al], axis=0), ch, NN)
        grad_down = tall[:blk] + (tall[blk:] + dot(ah, cl, NN))
        gh, gl = split(grad_pre.T)
        tall = dot(jnp.concatenate([gh, gl], axis=0), xh, NN)
        grad_up = tall[:blk] + (tall[blk:] + dot(gh, xl, NN))
        ph, plow = split(grad_pre)
        back = dot(jnp.concatenate([ph, plow], axis=1), jnp.concatenate([uh, uh], axis=1), NT)
        back = back + dot(ph, ul, NT)
        for k in range(kb):
            part = slice(k * blk, (k + 1) * blk)
            g[0, f, k] = grad_up[:, part].T
            g[1, f, k] = grad_down[:, part]
            at = up_at[f * kb + k]
            acc[at] = acc[at] + back[:, part]
        return carry

    lax.fori_loop(0, fc, step, 0)
    for r in range(n):
        grad_copy(r).start()
    if last:
        span = nb // heads
        copies = []
        for r in range(heads):
            src = acc.at[pl.ds((hid ^ r) * span, span)]
            for half in range(2):
                copies.append(pltpu.make_async_copy(
                    src.at[:, pl.ds(half * rows, rows)],
                    outs[r % 2].at[r // 2, half],
                    i_sem.at[2 * r + half]))
    else:
        copies = [pltpu.make_async_copy(acc, outs[0], i_sem.at[0])]
    for copy in copies:
        copy.start()
    for copy in copies:
        copy.wait()
    for r in range(n):
        grad_copy(r).wait()


def block_pass(x, cot, got, parts, up_at, down_at, me, hid, heads, prev, last):
    tok = len(parts)
    _, fc, kb, q, blk = parts[0].shape
    rows, width = x.shape
    nb = width // blk
    direct = q % 8 == 0
    order = me ^ jnp.arange(tok, dtype=jnp.int32)
    if not direct:
        whole = jnp.take(jnp.stack(parts), order, axis=0)
        parts = [jnp.moveaxis(whole, 0, 3).reshape(2, fc, kb, blk, blk)]
    n, q_in = len(parts), parts[0].shape[3]
    first = prev is None
    cfg = (fc, kb, blk, rows, nb, n, q_in, heads, first, last)
    if n > 1:
        out = [jax.ShapeDtypeStruct((n // 2, 2, fc, kb, q_in, blk), F32)] * 2
    else:
        out = [jax.ShapeDtypeStruct((1, 2, fc, kb, blk, blk), F32)]
    if last:
        out += [jax.ShapeDtypeStruct((heads // 2, 2, nb // heads, rows, blk), F32)] * 2
    else:
        out += [jax.ShapeDtypeStruct((nb, 2 * rows, blk), F32)]
    operands = [x, cot, got] + parts + ([] if first else [prev])
    anywhere = pl.BlockSpec(memory_space=pl.ANY)
    products = 2 * rows * fc * kb * blk * blk
    results = pl.pallas_call(
        functools.partial(kernel, cfg),
        out_shape=out,
        grid_spec=pltpu.PrefetchScalarGridSpec(
            num_scalar_prefetch=3,
            grid=(1,),
            in_specs=[anywhere] * len(operands),
            out_specs=[anywhere] * len(out),
            scratch_shapes=[
                pltpu.VMEM((2, fc, kb, blk, blk), F32),
                pltpu.VMEM((2, fc, kb, blk, blk), F32),
                pltpu.VMEM((2, kb, 2 * rows, blk), F32),
                pltpu.VMEM((2, kb, 2 * rows, blk), F32),
                pltpu.VMEM((nb, 2 * rows, blk), F32),
                pltpu.SemaphoreType.DMA((n,)),
                pltpu.SemaphoreType.DMA((n,)),
                pltpu.SemaphoreType.DMA((2, 4 * kb)),
                pltpu.SemaphoreType.DMA((2 * heads,)),
            ],
        ),
        compiler_params=pltpu.CompilerParams(vmem_limit_bytes=48 * 2**20),
        cost_estimate=pl.CostEstimate(
            flops=2 * 5 * 3 * products, bytes_accessed=16 * 2**20, transcendentals=0),
    )(up_at.reshape(-1), down_at.reshape(-1), jnp.stack([me, hid]), *operands)
    if n > 1:
        grads, rest = results[:2], results[2:]
    else:
        whole = results[0].reshape(2, fc, kb, tok, q, blk)
        whole = jnp.take(jnp.moveaxis(whole, 3, 0), order, axis=0)
        whole = whole.reshape((tok // 2, 2) + whole.shape[1:])
        grads, rest = (whole[:, 0], whole[:, 1]), results[1:]
    return grads, rest


def shards(inputs, cotangent, up_blocks, down_blocks, up_index, down_index, mom_up, mom_down):
    rows, width = inputs.shape
    blocks, kb, q, blk = up_blocks.shape
    tok, heads = lax.axis_size("tok"), lax.axis_size("hid")
    me, hid = lax.axis_index("tok"), lax.axis_index("hid")
    inner = inner_size(tok)
    pair = inner
    spread = [b for b in reversed(bits_below(tok)) if b != pair]
    half = blocks // 2
    chunks = 2 if half > 8 else 1
    fc = half // chunks
    side = (me // pair) % 2
    scale = (rows * tok) ** (-0.5)

    span = width // heads
    both = jnp.stack([
        lax.dynamic_slice(a, (0, hid * span), (rows, span)) for a in (inputs, cotangent)])
    pieces = {0: swap(both, "tok", pair)}
    for bit in reversed(bits_below(heads)):
        for r in list(pieces):
            pieces[r | bit] = swap(pieces[r], "hid", bit)
    got = jnp.zeros((2, rows, width), F32)
    for r, piece in pieces.items():
        got = lax.dynamic_update_slice(got, piece, (0, 0, (hid ^ r) * span))

    def weights(which, c):
        at = which * half + c * fc
        return jnp.stack([
            lax.dynamic_slice(a, (at, 0, 0, 0), (fc, kb, q, blk)) for a in (up_blocks, down_blocks)])

    grads = []
    partial = None
    for c in range(chunks):
        parts = {0: weights(side, c), pair: swap(weights(1 - side, c), "tok", pair)}
        for bit in spread:
            for r in list(parts):
                parts[r | bit] = swap(parts[r], "tok", bit)
        at = (side * half + c * fc, 0)
        (g0, g1), rest = block_pass(
            inputs, cotangent, got, [parts[r] for r in range(tok)],
            lax.dynamic_slice(up_index, at, (fc, kb)),
            lax.dynamic_slice(down_index, at, (fc, kb)),
            me, hid, heads, partial, c == chunks - 1)
        partial = rest[0]

        total = g0 + swap(g1, "tok", 1) if pair != 1 else None
        names = [b for b in reversed(bits_below(tok)) if b != 1]
        shape = total.shape[1:]
        total = total.reshape((2,) * len(names) + shape)
        for bit in reversed(spread[:-1]):
            axis = names.index(bit)
            keep = lax.index_in_dim(total, 0, axis, keepdims=False)
            send = lax.index_in_dim(total, 1, axis, keepdims=False)
            total = keep + swap(send, "tok", bit)
            names.remove(bit)
        grads.append((total[0], swap(total[1], "tok", pair)))

    even, odd = rest
    total = even + swap(odd, "hid", 1)
    for bit in bits_below(heads)[1:]:
        total = total.reshape((total.shape[0] // 2, 2) + total.shape[1:])
        total = total[:, 0] + swap(total[:, 1], "hid", bit)
    total = total[0, 0] + swap(total[0, 1], "tok", pair)
    input_grad = jnp.moveaxis(total, 0, 1).reshape(rows, span)

    mine = jnp.concatenate([a for a, _ in grads], axis=1)
    other = jnp.concatenate([b for _, b in grads], axis=1)
    ordered = jnp.concatenate(
        [jnp.where(side == 0, mine, other), jnp.where(side == 0, other, mine)], axis=1)
    return (
        input_grad,
        0.9 * mom_up + scale * ordered[0],
        0.9 * mom_down + scale * ordered[1],
    )


def solution(mesh):
    return jax.shard_map(
        shards,
        mesh=mesh,
        in_specs=(
            P("tok", None),
            P("tok", None),
            P("hid", None, "tok", None),
            P("hid", None, "tok", None),
            P("hid", None),
            P("hid", None),
            P("hid", None, "tok", None),
            P("hid", None, "tok", None),
        ),
        out_specs=(P("tok", "hid"), P("hid", None, "tok", None), P("hid", None, "tok", None)),
        check_vma=False,
    )
```

```python
import functools

import jax
import jax.numpy as jnp
from jax import lax
from jax.experimental import pallas as pl
from jax.experimental.pallas import tpu as pltpu
from jax.sharding import PartitionSpec as P

F32, BF16 = jnp.float32, jnp.bfloat16
NN = (((1,), (0,)), ((), ()))
NT = (((1,), (1,)), ((), ()))


def swap(value, axis, bit):
    size = lax.axis_size(axis)
    return lax.ppermute(value, axis, [(i, i ^ bit) for i in range(size)])


def bits_below(size):
    return [1 << i for i in range(size.bit_length() - 1)]


def inner_size(size):
    inner = 1
    while inner * inner * 8 <= size:
        inner *= 2
    return inner


def split(value):
    high = value.astype(BF16)
    return high, (value - high.astype(F32)).astype(BF16)


def dot(a, b, dims):
    return lax.dot_general(a, b, dims, preferred_element_type=F32)


def kernel(cfg, awaits, up_at, down_at, place, *refs):
    f0, fc, kb, blk, rows, nb, n, q, heads, first, last = cfg
    refs = list(refs)
    groups = min(n, 2)
    x_own, c_own, xc_got = refs[:3]
    slabs = refs[3:3 + n]
    refs = refs[3 + n:]
    prev = None
    if not first:
        prev, refs = refs[0], refs[1:]
    if awaits:
        refs = refs[1:]
    grads, refs = refs[:groups], refs[groups:]
    out, w, g, xb, cb, acc, w_sem, g_sem, x_sem, i_sem = refs
    me = place[0]
    span = nb // heads

    def weight_copy(r):
        start = pl.multiple_of((me ^ r) * q, q) if n > 1 else 0
        return pltpu.make_async_copy(
            slabs[r].at[:, pl.ds(f0, fc)], w.at[:, :, :, pl.ds(start, q), :], w_sem.at[r])

    def grad_copy(r):
        start = pl.multiple_of((me ^ r) * q, q) if n > 1 else 0
        return pltpu.make_async_copy(g.at[:, :, :, pl.ds(start, q), :], grads[r % 2].at[r // 2], g_sem.at[r])

    def token_copies(f, slot):
        copies = []
        for k in range(kb):
            for i, (own, at, buf) in enumerate((
                (x_own, up_at[f * kb + k], xb), (c_own, down_at[f * kb + k], cb))):
                col = pl.multiple_of(at * blk, blk)
                got_col = pl.multiple_of(lax.rem(at, span) * blk, blk)
                got = xc_got.at[lax.div(at, span), i]
                copies.append(pltpu.make_async_copy(
                    own.at[:, pl.ds(col, blk)], buf.at[slot, k, pl.ds(0, rows)],
                    x_sem.at[slot, 4 * k + 2 * i]))
                copies.append(pltpu.make_async_copy(
                    got.at[:, pl.ds(got_col, blk)], buf.at[slot, k, pl.ds(rows, rows)],
                    x_sem.at[slot, 4 * k + 2 * i + 1]))
        return copies

    for r in range(n):
        weight_copy(r).start()
    for copy in token_copies(0, 0):
        copy.start()
    if first:
        acc[...] = jnp.zeros_like(acc)
    else:
        fill = pltpu.make_async_copy(prev, acc, i_sem.at[0])
        fill.start()
        fill.wait()
    for r in range(n):
        weight_copy(r).wait()

    def step(f, carry):
        slot = lax.rem(f, 2)

        @pl.when(f + 1 < fc)
        def _():
            for copy in token_copies(f + 1, 1 - slot):
                copy.start()

        for copy in token_copies(f, slot):
            copy.wait()
        xh, xl = split(jnp.concatenate([xb[slot, k] for k in range(kb)], axis=1))
        ch, cl = split(jnp.concatenate([cb[slot, k] for k in range(kb)], axis=1))
        uh, ul = split(w[0, f].reshape(kb * blk, blk))
        dh, dl = split(jnp.concatenate([w[1, f, k] for k in range(kb)], axis=1))

        wide = dot(xh, jnp.concatenate([uh, ul], axis=1), NN)
        pre = wide[:, :blk] + (wide[:, blk:] + dot(xl, uh, NN))
        wide = dot(ch, jnp.concatenate([dh, dl], axis=0), NT)
        grad_act = wide[:, :blk] + (wide[:, blk:] + dot(cl, dh, NT))
        sig = jax.nn.sigmoid(pre)
        act = pre * sig
        grad_pre = grad_act * sig * (1.0 + pre * (1.0 - sig))

        ah, al = split(act.T)
        tall = dot(jnp.concatenate([ah, al], axis=0), ch, NN)
        grad_down = tall[:blk] + (tall[blk:] + dot(ah, cl, NN))
        gh, gl = split(grad_pre.T)
        tall = dot(jnp.concatenate([gh, gl], axis=0), xh, NN)
        grad_up = tall[:blk] + (tall[blk:] + dot(gh, xl, NN))
        ph, plow = split(grad_pre)
        back = dot(jnp.concatenate([ph, plow], axis=1), jnp.concatenate([uh, uh], axis=1), NT)
        back = back + dot(ph, ul, NT)
        for k in range(kb):
            part = slice(k * blk, (k + 1) * blk)
            g[0, f, k] = grad_up[:, part].T
            g[1, f, k] = grad_down[:, part]
            at = up_at[f * kb + k]
            acc[at] = acc[at] + back[:, part]
        return carry

    lax.fori_loop(0, fc, step, 0)
    for r in range(n):
        grad_copy(r).start()
    if last:
        copies = []
        for j in range(nb):
            for half in range(2):
                copies.append(pltpu.make_async_copy(
                    acc.at[j, pl.ds(half * rows, rows)],
                    out.at[j // span, half, :, pl.ds(j % span * blk, blk)],
                    i_sem.at[2 * j + half]))
    else:
        copies = [pltpu.make_async_copy(acc, out, i_sem.at[0])]
    for copy in copies:
        copy.start()
    for copy in copies:
        copy.wait()
    for r in range(n):
        grad_copy(r).wait()


def block_pass(x, cot, got, parts, f0, up_at, down_at, me, tok, heads, prev, last, awaits):
    fc = up_at.shape[0]
    n = len(parts)
    kb, q, blk = parts[0].shape[2:]
    rows, width = x.shape
    nb = width // blk
    first = prev is None
    cfg = (f0, fc, kb, blk, rows, nb, n, q, heads, first, last)
    groups = min(n, 2)
    out = [jax.ShapeDtypeStruct((n // groups, 2, fc, kb, q, blk), F32)] * groups
    if last:
        out.append(jax.ShapeDtypeStruct((heads, 2, rows, width // heads), F32))
    else:
        out.append(jax.ShapeDtypeStruct((nb, 2 * rows, blk), F32))
    operands = [x, cot, got] + parts + ([] if first else [prev]) + awaits
    anywhere = pl.BlockSpec(memory_space=pl.ANY)
    products = 2 * rows * fc * kb * blk * blk
    results = pl.pallas_call(
        functools.partial(kernel, cfg, len(awaits)),
        out_shape=out,
        grid_spec=pltpu.PrefetchScalarGridSpec(
            num_scalar_prefetch=3,
            grid=(1,),
            in_specs=[anywhere] * len(operands),
            out_specs=[anywhere] * len(out),
            scratch_shapes=[
                pltpu.VMEM((2, fc, kb, blk, blk), F32),
                pltpu.VMEM((2, fc, kb, blk, blk), F32),
                pltpu.VMEM((2, kb, 2 * rows, blk), F32),
                pltpu.VMEM((2, kb, 2 * rows, blk), F32),
                pltpu.VMEM((nb, 2 * rows, blk), F32),
                pltpu.SemaphoreType.DMA((n,)),
                pltpu.SemaphoreType.DMA((n,)),
                pltpu.SemaphoreType.DMA((2, 4 * kb)),
                pltpu.SemaphoreType.DMA((2 * nb,)),
            ],
        ),
        compiler_params=pltpu.CompilerParams(vmem_limit_bytes=40 * 2**20),
        cost_estimate=pl.CostEstimate(
            flops=8 * 5 * 3 * products, bytes_accessed=16 * 2**20, transcendentals=0),
    )(up_at.reshape(-1), down_at.reshape(-1), jnp.stack([me]), *operands)
    if n > 1:
        return results
    whole = results[0].reshape(2, fc, kb, tok, q // tok, blk)
    whole = jnp.take(jnp.moveaxis(whole, 3, 0), me ^ jnp.arange(tok), axis=0)
    whole = whole.reshape((tok // 2, 2) + whole.shape[1:])
    return whole[:, 0], whole[:, 1], results[-1]


def after(value, *others):
    return lax.optimization_barrier((value, *others))[0]


def shards(inputs, cotangent, up_blocks, down_blocks, up_index, down_index, mom_up, mom_down):
    rows, width = inputs.shape
    blocks, kb, q, blk = up_blocks.shape
    tok, heads = lax.axis_size("tok"), lax.axis_size("hid")
    me, hid = lax.axis_index("tok"), lax.axis_index("hid")
    inner = inner_size(tok)
    pair = inner
    near = bits_below(inner)
    far = [b for b in range(0, tok, 2 * inner)]
    half = blocks // 2
    chunks = 2 if half > 8 else 1
    fc = half // chunks
    side = (me // pair) % 2
    scale = (rows * tok) ** (-0.5)
    span = width // heads

    def weights(which, c):
        at = which * half + c * fc
        return jnp.stack([
            lax.dynamic_slice(a, (at, 0, 0, 0), (fc, kb, q, blk)) for a in (up_blocks, down_blocks)])

    both = jnp.stack([
        lax.dynamic_slice(a, (0, hid * span), (rows, span)) for a in (inputs, cotangent)])
    fetched = swap(both, "tok", pair)

    gathered = []
    for c in range(chunks):
        mine, other = weights(side, c), weights(1 - side, c)
        parts = {0: mine}
        for r in far:
            for source, to in ((mine, r), (other, r | pair)):
                if to:
                    if c:
                        source = after(source, gathered[c - 1][to])
                    parts[to] = swap(source, "tok", to)
        if c == 0:
            fetched = after(fetched, parts[pair], parts[far[-1]])
        for bit in near:
            for r in list(parts):
                parts[r | bit] = swap(parts[r], "tok", bit)
        gathered.append(parts)
    got = lax.all_gather(fetched, "hid")

    totals = []
    partial = None
    received = []
    for c in range(chunks):
        parts = [gathered[c][r] for r in range(tok)]
        if q % 8:
            whole = jnp.take(jnp.stack(parts), me ^ jnp.arange(tok), axis=0)
            parts = [jnp.moveaxis(whole, 0, 3).reshape(2, fc, kb, blk, blk)]
        cuts = [0, (fc + 1) // 2, fc]
        for p, (f0, f1) in enumerate(zip(cuts[:-1], cuts[1:])):
            at = (side * half + c * fc + f0, 0)
            even, odd, partial = block_pass(
                inputs, cotangent, got, parts, f0,
                lax.dynamic_slice(up_index, at, (f1 - f0, kb)),
                lax.dynamic_slice(down_index, at, (f1 - f0, kb)),
                me, tok, heads, partial, c == chunks - 1 and f1 == fc,
                [received[p]] if c else [])

            got_back = swap(odd, "tok", 1)
            received.append(got_back)
            sums = {2 * i: even[i] + got_back[i] for i in reversed(range(tok // 2))}
            for bit in near[1:]:
                for r in [r for r in sums if not r & bit]:
                    sums[r] = sums[r] + swap(sums.pop(r | bit), "tok", bit)
            totals.append(sums)

    mine, other = [], []
    for sums in totals:
        back = {r: swap(sums[r], "tok", r) for r in sorted(sums, reverse=True) if r}
        mine.append(sums[0] + sum(back[r] for r in far if r))
        other.append(sum(back[r | pair] for r in far))

    share = lax.psum_scatter(partial, "hid", scatter_dimension=0)
    input_grad = share[0] + swap(share[1], "tok", pair)

    mine, other = jnp.concatenate(mine, axis=1), jnp.concatenate(other, axis=1)
    ordered = jnp.concatenate(
        [jnp.where(side == 0, mine, other), jnp.where(side == 0, other, mine)], axis=1)
    return (
        input_grad,
        0.9 * mom_up + scale * ordered[0],
        0.9 * mom_down + scale * ordered[1],
    )


def solution(mesh):
    return jax.shard_map(
        shards,
        mesh=mesh,
        in_specs=(
            P("tok", None),
            P("tok", None),
            P("hid", None, "tok", None),
            P("hid", None, "tok", None),
            P("hid", None),
            P("hid", None),
            P("hid", None, "tok", None),
            P("hid", None, "tok", None),
        ),
        out_specs=(P("tok", "hid"), P("hid", None, "tok", None), P("hid", None, "tok", None)),
        check_vma=False,
    )
```

```python
import functools

import jax
import jax.numpy as jnp
from jax import lax
from jax.experimental import pallas as pl
from jax.experimental.pallas import tpu as pltpu
from jax.sharding import PartitionSpec as P

F32, BF16 = jnp.float32, jnp.bfloat16
NN = (((1,), (0,)), ((), ()))
NT = (((1,), (1,)), ((), ()))


def swap(value, axis, bit):
    size = lax.axis_size(axis)
    return lax.ppermute(value, axis, [(i, i ^ bit) for i in range(size)])


def bits_below(size):
    return [1 << i for i in range(size.bit_length() - 1)]


def inner_size(size):
    inner = 1
    while inner * inner * 8 <= size:
        inner *= 2
    return inner


def split(value):
    high = value.astype(BF16)
    return high, (value - high.astype(F32)).astype(BF16)


def dot(a, b, dims):
    return lax.dot_general(a, b, dims, preferred_element_type=F32)


def kernel(cfg, up_at, down_at, place, *refs):
    starts, sizes, kb, blk, rows, nb, n, q, heads, first, last, awaits = cfg
    fc = sum(sizes)
    refs = list(refs)
    groups = min(n, 2)
    x_own, c_own = refs[:2]
    got, refs = refs[2:2 + heads], refs[2 + heads:]
    slabs, refs = refs[:n], refs[n:]
    prev = None
    if not first:
        prev, refs = refs[0], refs[1:]
    refs = refs[awaits:]
    grads = []
    for _ in sizes:
        grads.append(refs[:groups])
        refs = refs[groups:]
    outs, refs = refs[:4 if last else 1], refs[4 if last else 1:]
    w, g, xb, cb, acc, w_sem, g_sem, x_sem, i_sem = refs
    me, hid = place[0], place[1]
    span = nb // heads

    def weight_copy(r):
        start = pl.multiple_of((me ^ r) * q, q) if n > 1 else 0
        return pltpu.make_async_copy(
            slabs[r].at[:, pl.ds(starts[r], fc)], w.at[:, :, :, pl.ds(start, q), :], w_sem.at[r])

    def grad_copies(act):
        for r in range(n):
            start = pl.multiple_of((me ^ r) * q, q) if n > 1 else 0
            f0 = 0
            for p, size in enumerate(sizes):
                act(pltpu.make_async_copy(
                    g.at[:, pl.ds(f0, size), :, pl.ds(start, q), :],
                    grads[p][r % 2].at[r // 2], g_sem.at[p, r]))
                f0 += size

    def token_copies(f, slot, act):
        for k in range(kb):
            for i, (own, ats, buf) in enumerate(((x_own, up_at, xb), (c_own, down_at, cb))):
                at = ats[f * kb + k]
                col = pl.multiple_of(at * blk, blk)
                act(pltpu.make_async_copy(
                    own.at[:, pl.ds(col, blk)], buf.at[slot, k, pl.ds(0, rows)],
                    x_sem.at[slot, 4 * k + 2 * i]))
                col = pl.multiple_of(lax.rem(at, span) * blk, blk)
                holder = lax.div(at, span) ^ hid
                for r in range(heads):
                    @pl.when(holder == r)
                    def _():
                        act(pltpu.make_async_copy(
                            got[r].at[i, :, pl.ds(col, blk)],
                            buf.at[slot, k, pl.ds(rows, rows)],
                            x_sem.at[slot, 4 * k + 2 * i + 1]))

    def start(copy):
        copy.start()

    def wait(copy):
        copy.wait()

    for r in range(n):
        weight_copy(r).start()
    token_copies(0, 0, start)
    if first:
        acc[...] = jnp.zeros_like(acc)
    else:
        fill = pltpu.make_async_copy(prev, acc, i_sem.at[0])
        fill.start()
        fill.wait()
    for r in range(n):
        weight_copy(r).wait()

    def step(f, carry):
        slot = lax.rem(f, 2)

        @pl.when(f + 1 < fc)
        def _():
            token_copies(f + 1, 1 - slot, start)

        token_copies(f, slot, wait)
        xh, xl = split(jnp.concatenate([xb[slot, k] for k in range(kb)], axis=1))
        ch, cl = split(jnp.concatenate([cb[slot, k] for k in range(kb)], axis=1))
        uh, ul = split(w[0, f].reshape(kb * blk, blk))
        dh, dl = split(jnp.concatenate([w[1, f, k] for k in range(kb)], axis=1))

        wide = dot(xh, jnp.concatenate([uh, ul], axis=1), NN)
        pre = wide[:, :blk] + (wide[:, blk:] + dot(xl, uh, NN))
        wide = dot(ch, jnp.concatenate([dh, dl], axis=0), NT)
        grad_act = wide[:, :blk] + (wide[:, blk:] + dot(cl, dh, NT))
        sig = jax.nn.sigmoid(pre)
        act = pre * sig
        grad_pre = grad_act * sig * (1.0 + pre * (1.0 - sig))

        ah, al = split(act.T)
        tall = dot(jnp.concatenate([ah, al], axis=0), ch, NN)
        grad_down = tall[:blk] + (tall[blk:] + dot(ah, cl, NN))
        gh, gl = split(grad_pre.T)
        tall = dot(jnp.concatenate([gh, gl], axis=0), xh, NN)
        grad_up = tall[:blk] + (tall[blk:] + dot(gh, xl, NN))
        ph, plow = split(grad_pre)
        back = dot(jnp.concatenate([ph, plow], axis=1), jnp.concatenate([uh, uh], axis=1), NT)
        back = back + dot(ph, ul, NT)
        for k in range(kb):
            part = slice(k * blk, (k + 1) * blk)
            g[0, f, k] = grad_up[:, part].T
            g[1, f, k] = grad_down[:, part]
            at = up_at[f * kb + k]
            acc[at] = acc[at] + back[:, part]
        return carry

    lax.fori_loop(0, fc, step, 0)
    grad_copies(start)
    if last:
        copies = []
        for r in range(heads):
            for j in range(span):
                for side in range(2):
                    copies.append(pltpu.make_async_copy(
                        acc.at[(hid ^ r) * span + j, pl.ds(side * rows, rows)],
                        outs[2 * side + r % 2].at[r // 2, :, pl.ds(j * blk, blk)],
                        i_sem.at[len(copies)]))
    else:
        copies = [pltpu.make_async_copy(acc, outs[0], i_sem.at[0])]
    for copy in copies:
        copy.start()
    for copy in copies:
        copy.wait()
    grad_copies(wait)


def block_pass(x, cot, got, slabs, up_at, down_at, me, hid, tok, heads, prev, sizes, last, awaits):
    fc = up_at.shape[0]
    n = len(slabs)
    starts, parts = zip(*slabs)
    kb, q, blk = parts[0].shape[2:]
    rows, width = x.shape
    nb = width // blk
    first = prev is None
    cfg = (starts, sizes, kb, blk, rows, nb, n, q, heads, first, last, len(awaits))
    groups = min(n, 2)
    out = [jax.ShapeDtypeStruct((n // groups, 2, size, kb, q, blk), F32)
           for size in sizes for _ in range(groups)]
    if last:
        out += [jax.ShapeDtypeStruct((heads // 2, rows, width // heads), F32)] * 4
    else:
        out.append(jax.ShapeDtypeStruct((nb, 2 * rows, blk), F32))
    operands = [x, cot] + got + list(parts) + ([] if first else [prev]) + awaits
    anywhere = pl.BlockSpec(memory_space=pl.ANY)
    products = 2 * rows * fc * kb * blk * blk
    results = pl.pallas_call(
        functools.partial(kernel, cfg),
        out_shape=out,
        grid_spec=pltpu.PrefetchScalarGridSpec(
            num_scalar_prefetch=3,
            grid=(1,),
            in_specs=[anywhere] * len(operands),
            out_specs=[anywhere] * len(out),
            scratch_shapes=[
                pltpu.VMEM((2, fc, kb, blk, blk), F32),
                pltpu.VMEM((2, fc, kb, blk, blk), F32),
                pltpu.VMEM((2, kb, 2 * rows, blk), F32),
                pltpu.VMEM((2, kb, 2 * rows, blk), F32),
                pltpu.VMEM((nb, 2 * rows, blk), F32),
                pltpu.SemaphoreType.DMA((n,)),
                pltpu.SemaphoreType.DMA((len(sizes), n)),
                pltpu.SemaphoreType.DMA((2, 4 * kb)),
                pltpu.SemaphoreType.DMA((2 * nb,)),
            ],
        ),
        compiler_params=pltpu.CompilerParams(vmem_limit_bytes=16 * 2**20),
        cost_estimate=pl.CostEstimate(
            flops=8 * 5 * 3 * products, bytes_accessed=16 * 2**20, transcendentals=0),
    )(up_at.reshape(-1), down_at.reshape(-1), jnp.stack([me, hid]), *operands)
    grads = []
    for p, size in enumerate(sizes):
        pair = results[p * groups:(p + 1) * groups]
        if n == 1:
            whole = pair[0].reshape(2, size, kb, tok, q // tok, blk)
            whole = jnp.take(jnp.moveaxis(whole, 3, 0), me ^ jnp.arange(tok), axis=0)
            whole = whole.reshape((tok // 2, 2) + whole.shape[1:])
            pair = whole[:, 0], whole[:, 1]
        grads.append(pair)
    return grads, results[len(sizes) * groups:]


def after(value, *others):
    return lax.optimization_barrier((value, *others))[0]


def shards(inputs, cotangent, up_blocks, down_blocks, up_index, down_index, mom_up, mom_down):
    rows, width = inputs.shape
    blocks, kb, q, blk = up_blocks.shape
    tok, heads = lax.axis_size("tok"), lax.axis_size("hid")
    me, hid = lax.axis_index("tok"), lax.axis_index("hid")
    inner = inner_size(tok)
    pair = inner
    near = bits_below(inner)
    far = [b for b in range(0, tok, 2 * inner)]
    half = blocks // 2
    cuts = [round(half * part / 14) for part in (0, 3, 7, 11, 14)]
    edges = [0, cuts[2], half]
    calls = [cuts[:2], cuts[1:3], cuts[2:]]
    side = (me // pair) % 2
    scale = (rows * tok) ** (-0.5)
    span = width // heads

    def weights(which, f0, f1):
        at = which * half + f0
        return jnp.stack([
            lax.dynamic_slice(a, (at, 0, 0, 0), (f1 - f0, kb, q, blk))
            for a in (up_blocks, down_blocks)])

    both = jnp.stack([
        lax.dynamic_slice(a, (0, hid * span), (rows, span)) for a in (inputs, cotangent)])
    tokens = swap(both, "tok", pair)
    mine, other = weights(side, 0, half), weights(1 - side, 0, half)
    parts = {0: [(0, mine)], far[-1] | pair: [(0, swap(other, "tok", far[-1] | pair))]}
    for r in far:
        for which, to in ((side, r), (1 - side, r | pair)):
            if to not in parts:
                parts[to] = []
                for f0, f1 in zip(edges[:-1], edges[1:]):
                    source = weights(which, f0, f1)
                    if f0:
                        source = after(source, parts[to][0][1])
                    parts[to].append((f0, swap(source, "tok", to)))
    first_in = [parts[r][0][1] for r in parts if r and len(parts[r]) > 1]
    for bit in near:
        for r in list(parts):
            parts[r | bit] = [(f0, swap(part, "tok", bit)) for f0, part in parts[r]]

    before = [part for r in parts if r & 1 for f0, part in parts[r] if f0]

    pieces = {0: after(tokens, parts[far[-1] | pair][0][1], parts[1][0][1])}
    for bit in reversed(bits_below(heads)):
        for r in list(pieces):
            source = pieces[r]
            if bit == 1:
                source = after(source, *first_in, parts[far[-1] | pair | 1][0][1])
            pieces[r | bit] = swap(source, "hid", bit)
    got = [pieces[r] for r in range(heads)]

    mine, other = [], []
    partial = None
    returned = [[], []]
    crossed = []
    for call in calls:
        f0, f1 = call[0], call[-1]
        slabs = []
        for r in range(tok):
            start, part = [(start, part) for start, part in parts[r] if start <= f0][-1]
            slabs.append((f0 - start, part))
        if q % 8:
            whole = jnp.stack([part[:, at:at + f1 - f0] for at, part in slabs])
            whole = jnp.take(whole, me ^ jnp.arange(tok), axis=0)
            slabs = [(0, jnp.moveaxis(whole, 0, 3).reshape(2, f1 - f0, kb, blk, blk))]
        at = (side * half + f0, 0)
        grads, rest = block_pass(
            inputs, cotangent, got, slabs,
            lax.dynamic_slice(up_index, at, (f1 - f0, kb)),
            lax.dynamic_slice(down_index, at, (f1 - f0, kb)),
            me, hid, tok, heads, partial,
            [b - a for a, b in zip(call[:-1], call[1:])], f1 == half,
            crossed[:1] if f1 == half else [])
        partial = rest[0]

        for even, odd in grads:
            got_back = swap(after(odd, *before, *returned[0]), "tok", 1)
            before = [got_back]
            crossed.append(got_back)
            sums = {2 * i: even[i] + got_back[i] for i in reversed(range(tok // 2))}
            for bit in near[1:]:
                for r in [r for r in sums if not r & bit]:
                    sums[r] = sums[r] + swap(sums.pop(r | bit), "tok", bit)
            back = {r: swap(sums[r], "tok", r) for r in sorted(sums, reverse=True) if r}
            returned = [returned[1], list(back.values())]
            mine.append(sums[0] + sum(back[r] for r in far if r))
            other.append(sum(back[r | pair] for r in far))

    shares = []
    for side_rows in range(2):
        even, odd = rest[2 * side_rows:2 * side_rows + 2]
        total = even + after(swap(odd, "hid", 1), crossed[2])
        for bit in bits_below(heads)[1:]:
            total = total.reshape((total.shape[0] // 2, 2) + total.shape[1:])
            total = total[:, 0] + swap(total[:, 1], "hid", bit)
        shares.append(total[0])
    input_grad = shares[0] + swap(shares[1], "tok", pair)

    mine, other = jnp.concatenate(mine, axis=1), jnp.concatenate(other, axis=1)
    ordered = jnp.concatenate(
        [jnp.where(side == 0, mine, other), jnp.where(side == 0, other, mine)], axis=1)
    return (
        input_grad,
        0.9 * mom_up + scale * ordered[0],
        0.9 * mom_down + scale * ordered[1],
    )


def solution(mesh):
    return jax.shard_map(
        shards,
        mesh=mesh,
        in_specs=(
            P("tok", None),
            P("tok", None),
            P("hid", None, "tok", None),
            P("hid", None, "tok", None),
            P("hid", None),
            P("hid", None),
            P("hid", None, "tok", None),
            P("hid", None, "tok", None),
        ),
        out_specs=(P("tok", "hid"), P("hid", None, "tok", None), P("hid", None, "tok", None)),
        check_vma=False,
    )
```

```python
import functools

import jax
import jax.numpy as jnp
from jax import lax
from jax.experimental import pallas as pl
from jax.experimental.pallas import tpu as pltpu
from jax.sharding import PartitionSpec as P

F32, BF16 = jnp.float32, jnp.bfloat16
NN = (((1,), (0,)), ((), ()))
NT = (((1,), (1,)), ((), ()))


def swap(value, axis, bit):
    size = lax.axis_size(axis)
    return lax.ppermute(value, axis, [(i, i ^ bit) for i in range(size)])


def bits_below(size):
    return [1 << i for i in range(size.bit_length() - 1)]


def inner_size(size):
    inner = 1
    while inner * inner * 8 <= size:
        inner *= 2
    return inner


def split(value):
    high = value.astype(BF16)
    return high, (value - high.astype(F32)).astype(BF16)


def dot(a, b, dims):
    return lax.dot_general(a, b, dims, preferred_element_type=F32)


def kernel(cfg, up_at, down_at, place, *refs):
    starts, sizes, kb, blk, rows, nb, n, q, heads, first, last, awaits = cfg
    fc = sum(sizes)
    refs = list(refs)
    groups = min(n, 2)
    x_own, c_own = refs[:2]
    got, refs = refs[2:2 + heads], refs[2 + heads:]
    slabs, refs = refs[:n], refs[n:]
    prev = None
    if not first:
        prev, refs = refs[0], refs[1:]
    refs = refs[awaits:]
    grads = []
    for _ in sizes:
        grads.append(refs[:groups])
        refs = refs[groups:]
    outs, refs = refs[:4 if last else 1], refs[4 if last else 1:]
    w, g, xb, cb, acc, w_sem, g_sem, x_sem, i_sem = refs
    me, hid = place[0], place[1]
    span = nb // heads

    def weight_copy(r):
        start = pl.multiple_of((me ^ r) * q, q) if n > 1 else 0
        return pltpu.make_async_copy(
            slabs[r].at[:, pl.ds(starts[r], fc)], w.at[:, :, :, pl.ds(start, q), :], w_sem.at[r])

    def grad_copies(act):
        for r in range(n):
            start = pl.multiple_of((me ^ r) * q, q) if n > 1 else 0
            f0 = 0
            for p, size in enumerate(sizes):
                act(pltpu.make_async_copy(
                    g.at[:, pl.ds(f0, size), :, pl.ds(start, q), :],
                    grads[p][r % 2].at[r // 2], g_sem.at[p, r]))
                f0 += size

    def token_copies(f, slot, act):
        for k in range(kb):
            for i, (own, ats, buf) in enumerate(((x_own, up_at, xb), (c_own, down_at, cb))):
                at = ats[f * kb + k]
                col = pl.multiple_of(at * blk, blk)
                act(pltpu.make_async_copy(
                    own.at[:, pl.ds(col, blk)], buf.at[slot, k, pl.ds(0, rows)],
                    x_sem.at[slot, 4 * k + 2 * i]))
                col = pl.multiple_of(lax.rem(at, span) * blk, blk)
                holder = lax.div(at, span) ^ hid
                for r in range(heads):
                    @pl.when(holder == r)
                    def _():
                        act(pltpu.make_async_copy(
                            got[r].at[i, :, pl.ds(col, blk)],
                            buf.at[slot, k, pl.ds(rows, rows)],
                            x_sem.at[slot, 4 * k + 2 * i + 1]))

    def start(copy):
        copy.start()

    def wait(copy):
        copy.wait()

    for r in range(n):
        weight_copy(r).start()
    token_copies(0, 0, start)
    if first:
        acc[...] = jnp.zeros_like(acc)
    else:
        fill = pltpu.make_async_copy(prev, acc, i_sem.at[0])
        fill.start()
        fill.wait()
    for r in range(n):
        weight_copy(r).wait()

    def step(f, carry):
        slot = lax.rem(f, 2)

        @pl.when(f + 1 < fc)
        def _():
            token_copies(f + 1, 1 - slot, start)

        token_copies(f, slot, wait)
        xh, xl = split(jnp.concatenate([xb[slot, k] for k in range(kb)], axis=1))
        ch, cl = split(jnp.concatenate([cb[slot, k] for k in range(kb)], axis=1))
        uh, ul = split(w[0, f].reshape(kb * blk, blk))
        dh, dl = split(jnp.concatenate([w[1, f, k] for k in range(kb)], axis=1))

        wide = dot(xh, jnp.concatenate([uh, ul], axis=1), NN)
        pre = wide[:, :blk] + (wide[:, blk:] + dot(xl, uh, NN))
        wide = dot(ch, jnp.concatenate([dh, dl], axis=0), NT)
        grad_act = wide[:, :blk] + (wide[:, blk:] + dot(cl, dh, NT))
        sig = jax.nn.sigmoid(pre)
        act = pre * sig
        grad_pre = grad_act * sig * (1.0 + pre * (1.0 - sig))

        ah, al = split(act.T)
        tall = dot(jnp.concatenate([ah, al], axis=0), ch, NN)
        grad_down = tall[:blk] + (tall[blk:] + dot(ah, cl, NN))
        gh, gl = split(grad_pre.T)
        tall = dot(jnp.concatenate([gh, gl], axis=0), xh, NN)
        grad_up = tall[:blk] + (tall[blk:] + dot(gh, xl, NN))
        ph, plow = split(grad_pre)
        back = dot(jnp.concatenate([ph, plow], axis=1), jnp.concatenate([uh, uh], axis=1), NT)
        back = back + dot(ph, ul, NT)
        for k in range(kb):
            part = slice(k * blk, (k + 1) * blk)
            g[0, f, k] = grad_up[:, part].T
            g[1, f, k] = grad_down[:, part]
            at = up_at[f * kb + k]
            acc[at] = acc[at] + back[:, part]
        return carry

    lax.fori_loop(0, fc, step, 0)
    grad_copies(start)
    if last:
        copies = []
        for r in range(heads):
            for j in range(span):
                for side in range(2):
                    copies.append(pltpu.make_async_copy(
                        acc.at[(hid ^ r) * span + j, pl.ds(side * rows, rows)],
                        outs[2 * side + r % 2].at[r // 2, :, pl.ds(j * blk, blk)],
                        i_sem.at[len(copies)]))
    else:
        copies = [pltpu.make_async_copy(acc, outs[0], i_sem.at[0])]
    for copy in copies:
        copy.start()
    for copy in copies:
        copy.wait()
    grad_copies(wait)


def block_pass(x, cot, got, slabs, up_at, down_at, me, hid, tok, heads, prev, sizes, last, awaits):
    fc = up_at.shape[0]
    n = len(slabs)
    starts, parts = zip(*slabs)
    kb, q, blk = parts[0].shape[2:]
    rows, width = x.shape
    nb = width // blk
    first = prev is None
    cfg = (starts, sizes, kb, blk, rows, nb, n, q, heads, first, last, len(awaits))
    groups = min(n, 2)
    out = [jax.ShapeDtypeStruct((n // groups, 2, size, kb, q, blk), F32)
           for size in sizes for _ in range(groups)]
    if last:
        out += [jax.ShapeDtypeStruct((heads // 2, rows, width // heads), F32)] * 4
    else:
        out.append(pltpu.HBM((nb, 2 * rows, blk), F32))
    fixed = [pltpu.with_memory_space_constraint(a, pltpu.HBM)
             for a in [x, cot] + ([] if first else [prev])]
    operands = fixed[:2] + got + list(parts) + fixed[2:] + awaits
    anywhere = pl.BlockSpec(memory_space=pl.ANY)
    products = 2 * rows * fc * kb * blk * blk
    results = pl.pallas_call(
        functools.partial(kernel, cfg),
        out_shape=out,
        grid_spec=pltpu.PrefetchScalarGridSpec(
            num_scalar_prefetch=3,
            grid=(1,),
            in_specs=[anywhere] * len(operands),
            out_specs=[anywhere] * len(out),
            scratch_shapes=[
                pltpu.VMEM((2, fc, kb, blk, blk), F32),
                pltpu.VMEM((2, fc, kb, blk, blk), F32),
                pltpu.VMEM((2, kb, 2 * rows, blk), F32),
                pltpu.VMEM((2, kb, 2 * rows, blk), F32),
                pltpu.VMEM((nb, 2 * rows, blk), F32),
                pltpu.SemaphoreType.DMA((n,)),
                pltpu.SemaphoreType.DMA((len(sizes), n)),
                pltpu.SemaphoreType.DMA((2, 4 * kb)),
                pltpu.SemaphoreType.DMA((2 * nb,)),
            ],
        ),
        compiler_params=pltpu.CompilerParams(vmem_limit_bytes=16 * 2**20),
        cost_estimate=pl.CostEstimate(
            flops=8 * 5 * 3 * products, bytes_accessed=16 * 2**20, transcendentals=0),
    )(up_at.reshape(-1), down_at.reshape(-1), jnp.stack([me, hid]), *operands)
    grads = []
    for p, size in enumerate(sizes):
        pair = results[p * groups:(p + 1) * groups]
        if n == 1:
            whole = pair[0].reshape(2, size, kb, tok, q // tok, blk)
            whole = jnp.take(jnp.moveaxis(whole, 3, 0), me ^ jnp.arange(tok), axis=0)
            whole = whole.reshape((tok // 2, 2) + whole.shape[1:])
            pair = whole[:, 0], whole[:, 1]
        grads.append(pair)
    return grads, results[len(sizes) * groups:]


def after(value, *others):
    return lax.optimization_barrier((value, *others))[0]


def shards(inputs, cotangent, up_blocks, down_blocks, up_index, down_index, mom_up, mom_down):
    rows, width = inputs.shape
    blocks, kb, q, blk = up_blocks.shape
    tok, heads = lax.axis_size("tok"), lax.axis_size("hid")
    me, hid = lax.axis_index("tok"), lax.axis_index("hid")
    inner = inner_size(tok)
    pair = inner
    near = bits_below(inner)
    far = [b for b in range(0, tok, 2 * inner)]
    half = blocks // 2
    cuts = [round(half * part / 14) for part in (0, 3, 8, 11, 14)]
    edges = [0, cuts[2], half]
    calls = [cuts[:2], cuts[1:3], cuts[2:]]
    side = (me // pair) % 2
    scale = (rows * tok) ** (-0.5)
    span = width // heads

    def weights(which, f0, f1):
        at = which * half + f0
        return jnp.stack([
            lax.dynamic_slice(a, (at, 0, 0, 0), (f1 - f0, kb, q, blk))
            for a in (up_blocks, down_blocks)])

    both = jnp.stack([
        lax.dynamic_slice(a, (0, hid * span), (rows, span)) for a in (inputs, cotangent)])
    tokens = swap(both, "tok", pair)
    parts = {r: [] for r in range(tok)}

    def pass_on(r, f0, part):
        parts[r].append((f0, part))
        fresh = [(r, part)]
        for bit in near:
            fresh += [(to | bit, swap(got, "tok", bit)) for to, got in fresh]
        for to, got in fresh[1:]:
            parts[to].append((f0, got))
        return fresh[-1][1]

    own = pass_on(0, 0, weights(side, 0, half))
    waits, near_waits = [], [tokens]
    pieces = {}
    for f0, f1 in zip(edges[:-1], edges[1:]):
        mine, other = weights(side, f0, f1), weights(1 - side, f0, f1)
        for source, to in [(other, r | pair) for r in far if r] + [(mine, r) for r in far if r]:
            part = swap(after(source, *waits), "tok", to)
            passed = pass_on(to, f0, part)
            waits = [part]
            if f0 == 0 and to != far[-1]:
                early = passed
        if f0 == 0:
            pieces[0] = after(tokens, part, own, early)
            for bit in reversed(bits_below(heads)[1:]):
                for r in list(pieces):
                    pieces[r | bit] = swap(pieces[r], "hid", bit)
            pieces[1] = swap(after(pieces[0], passed), "hid", 1)
        part = swap(after(other, *near_waits), "tok", pair)
        pass_on(pair, f0, part)
        ends = [part, *waits]
        near_waits = [part, pieces[1]]
        if f0 == 0:
            held = part
    ends.append(parts[far[-1] | pair | 1][-1][1])
    crossed = [parts[pair | 1][-1][1], parts[far[-1] | 1][-1][1]]
    for r in range(2, heads, 2):
        pieces[r | 1] = swap(after(pieces[r], held, parts[far[-1] | pair][-1][1]), "hid", 1)
    got = [pieces[r] for r in range(heads)]

    mine, other = [], []
    partial = None
    returned = [[], []]
    for call in calls:
        f0, f1 = call[0], call[-1]
        slabs = []
        for r in range(tok):
            start, part = [(start, part) for start, part in parts[r] if start <= f0][-1]
            slabs.append((f0 - start, part))
        if q % 8:
            whole = jnp.stack([part[:, at:at + f1 - f0] for at, part in slabs])
            whole = jnp.take(whole, me ^ jnp.arange(tok), axis=0)
            slabs = [(0, jnp.moveaxis(whole, 0, 3).reshape(2, f1 - f0, kb, blk, blk))]
        at = (side * half + f0, 0)
        grads, rest = block_pass(
            inputs, cotangent, got, slabs,
            lax.dynamic_slice(up_index, at, (f1 - f0, kb)),
            lax.dynamic_slice(down_index, at, (f1 - f0, kb)),
            me, hid, tok, heads, partial,
            [b - a for a, b in zip(call[:-1], call[1:])], f1 == half,
            crossed[2:3] if f1 == half else ends if not f0 else [])
        partial = rest[0]

        for even, odd in grads:
            got_back = swap(after(odd, *crossed[-2 if len(crossed) == 2 else -1:], *returned[0]), "tok", 1)
            crossed.append(got_back)
            sums = {2 * i: even[i] + got_back[i] for i in reversed(range(tok // 2))}
            for bit in near[1:]:
                for r in [r for r in sums if not r & bit]:
                    sums[r] = sums[r] + swap(sums.pop(r | bit), "tok", bit)
            back = {r: swap(sums[r], "tok", r) for r in sorted(sums, reverse=True) if r}
            returned = [returned[1], list(back.values())]
            mine.append(sums[0] + sum(back[r] for r in far if r))
            other.append(sum(back[r | pair] for r in far))

    shares, first = [], []
    for side_rows in (1, 0):
        even, odd = rest[2 * side_rows:2 * side_rows + 2]
        total = even + after(swap(after(odd, *first), "hid", 1), crossed[4])
        first = [crossed[4]]
        for bit in bits_below(heads)[1:]:
            total = total.reshape((total.shape[0] // 2, 2) + total.shape[1:])
            total = total[:, 0] + swap(total[:, 1], "hid", bit)
        shares.append(total[0])
    input_grad = shares[1] + swap(shares[0], "tok", pair)

    mine, other = jnp.concatenate(mine, axis=1), jnp.concatenate(other, axis=1)
    ordered = jnp.concatenate(
        [jnp.where(side == 0, mine, other), jnp.where(side == 0, other, mine)], axis=1)
    return (
        input_grad,
        0.9 * mom_up + scale * ordered[0],
        0.9 * mom_down + scale * ordered[1],
    )


def solution(mesh):
    return jax.shard_map(
        shards,
        mesh=mesh,
        in_specs=(
            P("tok", None),
            P("tok", None),
            P("hid", None, "tok", None),
            P("hid", None, "tok", None),
            P("hid", None),
            P("hid", None),
            P("hid", None, "tok", None),
            P("hid", None, "tok", None),
        ),
        out_specs=(P("tok", "hid"), P("hid", None, "tok", None), P("hid", None, "tok", None)),
        check_vma=False,
    )
```

```python
import functools

import jax
import jax.numpy as jnp
from jax import lax
from jax.experimental import pallas as pl
from jax.experimental.pallas import tpu as pltpu
from jax.sharding import PartitionSpec as P

F32, BF16 = jnp.float32, jnp.bfloat16
NN = (((1,), (0,)), ((), ()))
NT = (((1,), (1,)), ((), ()))


def swap(value, axis, bit):
    size = lax.axis_size(axis)
    return lax.ppermute(value, axis, [(i, i ^ bit) for i in range(size)])


def bits_below(size):
    return [1 << i for i in range(size.bit_length() - 1)]


def inner_size(size):
    inner = 1
    while inner * inner * 8 <= size:
        inner *= 2
    return inner


def split(value):
    high = value.astype(BF16)
    return high, (value - high.astype(F32)).astype(BF16)


def dot(a, b, dims):
    return lax.dot_general(a, b, dims, preferred_element_type=F32)


def kernel(cfg, up_at, down_at, place, *refs):
    starts, sizes, kb, blk, rows, nb, n, q, heads, first, last, awaits = cfg
    fc = sum(sizes)
    refs = list(refs)
    groups = min(n, 2)
    x_own, c_own = refs[:2]
    got, refs = refs[2:2 + heads], refs[2 + heads:]
    slabs, refs = refs[:n], refs[n:]
    prev = None
    if not first:
        prev, refs = refs[0], refs[1:]
    refs = refs[awaits:]
    grads = []
    for _ in sizes:
        grads.append(refs[:groups])
        refs = refs[groups:]
    outs, refs = refs[:4 if last else 1], refs[4 if last else 1:]
    w, xb, cb, acc, w_sem, g_sem, x_sem, i_sem = refs
    me, hid = place[0], place[1]
    span = nb // heads

    def weight_copy(r):
        start = pl.multiple_of((me ^ r) * q, q) if n > 1 else 0
        return pltpu.make_async_copy(
            slabs[r].at[:, pl.ds(starts[r], fc)], w.at[:, :, :, pl.ds(start, q), :], w_sem.at[r])

    def grad_copies(act):
        for r in range(n):
            start = pl.multiple_of((me ^ r) * q, q) if n > 1 else 0
            f0 = 0
            for p, size in enumerate(sizes):
                act(pltpu.make_async_copy(
                    w.at[:, pl.ds(f0, size), :, pl.ds(start, q), :],
                    grads[p][r % 2].at[r // 2], g_sem.at[p, r]))
                f0 += size

    def token_copies(f, slot, act):
        for k in range(kb):
            for i, (own, ats, buf) in enumerate(((x_own, up_at, xb), (c_own, down_at, cb))):
                at = ats[f * kb + k]
                col = pl.multiple_of(at * blk, blk)
                act(pltpu.make_async_copy(
                    own.at[:, pl.ds(col, blk)], buf.at[slot, k, pl.ds(0, rows)],
                    x_sem.at[slot, 4 * k + 2 * i]))
                col = pl.multiple_of(lax.rem(at, span) * blk, blk)
                holder = lax.div(at, span) ^ hid
                for r in range(heads):
                    @pl.when(holder == r)
                    def _():
                        act(pltpu.make_async_copy(
                            got[r].at[i, :, pl.ds(col, blk)],
                            buf.at[slot, k, pl.ds(rows, rows)],
                            x_sem.at[slot, 4 * k + 2 * i + 1]))

    def start(copy):
        copy.start()

    def wait(copy):
        copy.wait()

    for r in range(n):
        weight_copy(r).start()
    token_copies(0, 0, start)
    if first:
        acc[...] = jnp.zeros_like(acc)
    else:
        fill = pltpu.make_async_copy(prev, acc, i_sem.at[0])
        fill.start()
        fill.wait()
    for r in range(n):
        weight_copy(r).wait()

    def step(f, carry):
        slot = lax.rem(f, 2)

        @pl.when(f + 1 < fc)
        def _():
            token_copies(f + 1, 1 - slot, start)

        token_copies(f, slot, wait)
        xh, xl = split(jnp.concatenate([xb[slot, k] for k in range(kb)], axis=1))
        ch, cl = split(jnp.concatenate([cb[slot, k] for k in range(kb)], axis=1))
        uh, ul = split(w[0, f].reshape(kb * blk, blk))
        dh, dl = split(jnp.concatenate([w[1, f, k] for k in range(kb)], axis=1))

        wide = dot(xh, jnp.concatenate([uh, ul], axis=1), NN)
        pre = wide[:, :blk] + (wide[:, blk:] + dot(xl, uh, NN))
        wide = dot(ch, jnp.concatenate([dh, dl], axis=0), NT)
        grad_act = wide[:, :blk] + (wide[:, blk:] + dot(cl, dh, NT))
        sig = jax.nn.sigmoid(pre)
        act = pre * sig
        grad_pre = grad_act * sig * (1.0 + pre * (1.0 - sig))

        ah, al = split(act.T)
        tall = dot(jnp.concatenate([ah, al], axis=0), ch, NN)
        grad_down = tall[:blk] + (tall[blk:] + dot(ah, cl, NN))
        gh, gl = split(grad_pre.T)
        tall = dot(jnp.concatenate([gh, gl], axis=0), xh, NN)
        grad_up = tall[:blk] + (tall[blk:] + dot(gh, xl, NN))
        ph, plow = split(grad_pre)
        back = dot(jnp.concatenate([ph, plow], axis=1), jnp.concatenate([uh, uh], axis=1), NT)
        back = back + dot(ph, ul, NT)
        for k in range(kb):
            part = slice(k * blk, (k + 1) * blk)
            w[0, f, k] = grad_up[:, part].T
            w[1, f, k] = grad_down[:, part]
            at = up_at[f * kb + k]
            acc[at] = acc[at] + back[:, part]
        return carry

    lax.fori_loop(0, fc, step, 0)
    grad_copies(start)
    if last:
        copies = []
        for r in range(heads):
            for j in range(span):
                for side in range(2):
                    copies.append(pltpu.make_async_copy(
                        acc.at[(hid ^ r) * span + j, pl.ds(side * rows, rows)],
                        outs[2 * side + r % 2].at[r // 2, :, pl.ds(j * blk, blk)],
                        i_sem.at[len(copies)]))
    else:
        copies = [pltpu.make_async_copy(acc, outs[0], i_sem.at[0])]
    for copy in copies:
        copy.start()
    for copy in copies:
        copy.wait()
    grad_copies(wait)


def block_pass(x, cot, got, slabs, up_at, down_at, me, hid, tok, heads, prev, sizes, last, awaits):
    fc = up_at.shape[0]
    n = len(slabs)
    starts, parts = zip(*slabs)
    kb, q, blk = parts[0].shape[2:]
    rows, width = x.shape
    nb = width // blk
    first = prev is None
    cfg = (starts, sizes, kb, blk, rows, nb, n, q, heads, first, last, len(awaits))
    groups = min(n, 2)
    out = [jax.ShapeDtypeStruct((n // groups, 2, size, kb, q, blk), F32)
           for size in sizes for _ in range(groups)]
    if last:
        out += [jax.ShapeDtypeStruct((heads // 2, rows, width // heads), F32)] * 4
    else:
        out.append(pltpu.HBM((nb, 2 * rows, blk), F32))
    fixed = [pltpu.with_memory_space_constraint(a, pltpu.HBM)
             for a in [x, cot] + ([] if first else [prev])]
    operands = fixed[:2] + got + list(parts) + fixed[2:] + awaits
    anywhere = pl.BlockSpec(memory_space=pl.ANY)
    products = 2 * rows * fc * kb * blk * blk
    results = pl.pallas_call(
        functools.partial(kernel, cfg),
        out_shape=out,
        grid_spec=pltpu.PrefetchScalarGridSpec(
            num_scalar_prefetch=3,
            grid=(1,),
            in_specs=[anywhere] * len(operands),
            out_specs=[anywhere] * len(out),
            scratch_shapes=[
                pltpu.VMEM((2, fc, kb, blk, blk), F32),
                pltpu.VMEM((2, kb, 2 * rows, blk), F32),
                pltpu.VMEM((2, kb, 2 * rows, blk), F32),
                pltpu.VMEM((nb, 2 * rows, blk), F32),
                pltpu.SemaphoreType.DMA((n,)),
                pltpu.SemaphoreType.DMA((len(sizes), n)),
                pltpu.SemaphoreType.DMA((2, 4 * kb)),
                pltpu.SemaphoreType.DMA((2 * nb,)),
            ],
        ),
        compiler_params=pltpu.CompilerParams(vmem_limit_bytes=13 * 2**20),
        cost_estimate=pl.CostEstimate(
            flops=8 * 5 * 3 * products, bytes_accessed=16 * 2**20, transcendentals=0),
    )(up_at.reshape(-1), down_at.reshape(-1), jnp.stack([me, hid]), *operands)
    grads = []
    for p, size in enumerate(sizes):
        pair = results[p * groups:(p + 1) * groups]
        if n == 1:
            whole = pair[0].reshape(2, size, kb, tok, q // tok, blk)
            whole = jnp.take(jnp.moveaxis(whole, 3, 0), me ^ jnp.arange(tok), axis=0)
            whole = whole.reshape((tok // 2, 2) + whole.shape[1:])
            pair = whole[:, 0], whole[:, 1]
        grads.append(pair)
    return grads, results[len(sizes) * groups:]


def after(value, *others):
    return lax.optimization_barrier((value, *others))[0]


def shards(inputs, cotangent, up_blocks, down_blocks, up_index, down_index, mom_up, mom_down):
    rows, width = inputs.shape
    blocks, kb, q, blk = up_blocks.shape
    tok, heads = lax.axis_size("tok"), lax.axis_size("hid")
    me, hid = lax.axis_index("tok"), lax.axis_index("hid")
    inner = inner_size(tok)
    pair = inner
    near = bits_below(inner)
    far = [b for b in range(0, tok, 2 * inner)]
    half = blocks // 2
    cuts = [round(half * part / 14) for part in (0, 3, 7, 11, 14)]
    edges = [0, cuts[2], half]
    calls = [cuts[:2], cuts[1:3], cuts[2:]]
    side = (me // pair) % 2
    scale = (rows * tok) ** (-0.5)
    span = width // heads

    def weights(which, f0, f1):
        at = which * half + f0
        return jnp.stack([
            lax.dynamic_slice(a, (at, 0, 0, 0), (f1 - f0, kb, q, blk))
            for a in (up_blocks, down_blocks)])

    both = jnp.stack([
        lax.dynamic_slice(a, (0, hid * span), (rows, span)) for a in (inputs, cotangent)])
    tokens = swap(both, "tok", pair)
    mine, other = weights(side, 0, half), weights(1 - side, 0, half)
    most = far[-1] | pair
    parts = {0: [(0, mine)], most: [(0, swap(other, "tok", most))]}
    for bit in near:
        for r in list(parts):
            parts[r | bit] = [(0, swap(parts[r][0][1], "tok", bit))]

    pieces = {0: after(tokens, parts[most][0][1], parts[1][0][1])}
    for bit in reversed(bits_below(heads)[1:]):
        for r in list(pieces):
            pieces[r | bit] = swap(pieces[r], "hid", bit)
    pieces[1] = swap(pieces[0], "hid", 1)

    sends = [(1 - side, pair)] + [
        send for r in far if r for send in ((side, r), (1 - side, r | pair)) if send[1] != most]
    for which, to in sends:
        for r in [to] + [to | bit for bit in range(1, inner)]:
            parts[r] = []
        for f0, f1 in zip(edges[:-1], edges[1:]):
            source = weights(which, f0, f1)
            if f0:
                source = after(source, parts[to][0][1], pieces[1])
            fresh = {to: swap(source, "tok", to)}
            for bit in near:
                fresh.update({r | bit: swap(part, "tok", bit) for r, part in fresh.items()})
            for r, part in fresh.items():
                parts[r].append((f0, part))
    before = [part for r in parts if r & 1 for f0, part in parts[r] if f0]
    held = [parts[to][0][1] for _, to in sends] + [parts[most | 1][0][1]]
    for r in range(2, heads, 2):
        pieces[r | 1] = swap(after(pieces[r], *held), "hid", 1)
    got = [pieces[r] for r in range(heads)]

    mine, other = [], []

    def finish(even, got_back):
        total = even + got_back
        left = [b for b in reversed(bits_below(tok)) if b != 1]
        for bit in near[1:] + [b for b in bits_below(tok) if b > pair]:
            p = left.index(bit)
            left.remove(bit)
            total = total.reshape((2 ** p, 2, -1) + total.shape[1:])
            back = swap(total[:, 1], "tok", bit)
            total = (total[:, 0] + back).reshape((-1,) + total.shape[3:])
        folded.append(back)
        mine.append(total[0])
        other.append(swap(total[1], "tok", pair))

    partial = None
    crossed, folded = [], []
    kept = None
    for call in calls:
        f0, f1 = call[0], call[-1]
        slabs = []
        for r in range(tok):
            start, part = [(start, part) for start, part in parts[r] if start <= f0][-1]
            slabs.append((f0 - start, part))
        if q % 8:
            whole = jnp.stack([part[:, at:at + f1 - f0] for at, part in slabs])
            whole = jnp.take(whole, me ^ jnp.arange(tok), axis=0)
            slabs = [(0, jnp.moveaxis(whole, 0, 3).reshape(2, f1 - f0, kb, blk, blk))]
        at = (side * half + f0, 0)
        grads, rest = block_pass(
            inputs, cotangent, got, slabs,
            lax.dynamic_slice(up_index, at, (f1 - f0, kb)),
            lax.dynamic_slice(down_index, at, (f1 - f0, kb)),
            me, hid, tok, heads, partial,
            [b - a for a, b in zip(call[:-1], call[1:])], f1 == half,
            crossed[:1] if f1 == half else [])
        partial = rest[0]
        if kept:
            finish(kept[0], after(kept[1], partial))
            kept = None

        for even, odd in grads:
            got_back = swap(after(odd, *before, *folded[-2:-1]), "tok", 1)
            before = [got_back]
            crossed.append(got_back)
            if len(crossed) == 2:
                kept = even, got_back
                continue
            finish(even, got_back)
    shares = []
    for side_rows in range(2):
        even, odd = rest[2 * side_rows:2 * side_rows + 2]
        total = even + after(swap(odd, "hid", 1), crossed[2])
        for bit in bits_below(heads)[1:]:
            total = total.reshape((total.shape[0] // 2, 2) + total.shape[1:])
            total = total[:, 0] + swap(total[:, 1], "hid", bit)
        shares.append(total[0])
    input_grad = shares[0] + swap(shares[1], "tok", pair)

    mine, other = jnp.concatenate(mine, axis=1), jnp.concatenate(other, axis=1)
    ordered = jnp.concatenate(
        [jnp.where(side == 0, mine, other), jnp.where(side == 0, other, mine)], axis=1)
    return (
        input_grad,
        0.9 * mom_up + scale * ordered[0],
        0.9 * mom_down + scale * ordered[1],
    )


def solution(mesh):
    return jax.shard_map(
        shards,
        mesh=mesh,
        in_specs=(
            P("tok", None),
            P("tok", None),
            P("hid", None, "tok", None),
            P("hid", None, "tok", None),
            P("hid", None),
            P("hid", None),
            P("hid", None, "tok", None),
            P("hid", None, "tok", None),
        ),
        out_specs=(P("tok", "hid"), P("hid", None, "tok", None), P("hid", None, "tok", None)),
        check_vma=False,
    )
```

```python
import functools

import jax
import jax.numpy as jnp
from jax import lax
from jax.experimental import pallas as pl
from jax.experimental.pallas import tpu as pltpu
from jax.sharding import PartitionSpec as P

F32, BF16 = jnp.float32, jnp.bfloat16
NN = (((1,), (0,)), ((), ()))
NT = (((1,), (1,)), ((), ()))


def swap(value, axis, bit):
    size = lax.axis_size(axis)
    return lax.ppermute(value, axis, [(i, i ^ bit) for i in range(size)])


def bits_below(size):
    return [1 << i for i in range(size.bit_length() - 1)]


def inner_size(size):
    inner = 1
    while inner * inner * 8 <= size:
        inner *= 2
    return inner


def split(value):
    high = value.astype(BF16)
    return high, (value - high.astype(F32)).astype(BF16)


def dot(a, b, dims):
    return lax.dot_general(a, b, dims, preferred_element_type=F32)


def kernel(cfg, up_at, down_at, place, *refs):
    starts, sizes, kb, blk, rows, nb, n, q, heads, first, last, awaits = cfg
    fc = sum(sizes)
    refs = list(refs)
    groups = min(n, 2)
    x_own, c_own = refs[:2]
    got, refs = refs[2:2 + heads], refs[2 + heads:]
    slabs, refs = refs[:n], refs[n:]
    prev = None
    if not first:
        prev, refs = refs[0], refs[1:]
    refs = refs[awaits:]
    grads = []
    for _ in sizes:
        grads.append(refs[:groups])
        refs = refs[groups:]
    outs, refs = refs[:4 if last else 1], refs[4 if last else 1:]
    w, xb, cb, acc, w_sem, g_sem, x_sem, i_sem = refs
    me, hid = place[0], place[1]
    span = nb // heads

    def weight_copy(r):
        start = pl.multiple_of((me ^ r) * q, q) if n > 1 else 0
        return pltpu.make_async_copy(
            slabs[r].at[:, pl.ds(starts[r], fc)], w.at[:, :, :, pl.ds(start, q), :], w_sem.at[r])

    def grad_copies(act):
        for r in range(n):
            start = pl.multiple_of((me ^ r) * q, q) if n > 1 else 0
            f0 = 0
            for p, size in enumerate(sizes):
                act(pltpu.make_async_copy(
                    w.at[:, pl.ds(f0, size), :, pl.ds(start, q), :],
                    grads[p][r % 2].at[r // 2], g_sem.at[p, r]))
                f0 += size

    def token_copies(f, slot, act):
        for k in range(kb):
            for i, (own, ats, buf) in enumerate(((x_own, up_at, xb), (c_own, down_at, cb))):
                at = ats[f * kb + k]
                col = pl.multiple_of(at * blk, blk)
                act(pltpu.make_async_copy(
                    own.at[:, pl.ds(col, blk)], buf.at[slot, k, pl.ds(0, rows)],
                    x_sem.at[slot, 4 * k + 2 * i]))
                col = pl.multiple_of(lax.rem(at, span) * blk, blk)
                holder = lax.div(at, span) ^ hid
                for r in range(heads):
                    @pl.when(holder == r)
                    def _():
                        act(pltpu.make_async_copy(
                            got[r].at[i, :, pl.ds(col, blk)],
                            buf.at[slot, k, pl.ds(rows, rows)],
                            x_sem.at[slot, 4 * k + 2 * i + 1]))

    def start(copy):
        copy.start()

    def wait(copy):
        copy.wait()

    for r in range(n):
        weight_copy(r).start()
    token_copies(0, 0, start)
    if first:
        acc[...] = jnp.zeros_like(acc)
    else:
        fill = pltpu.make_async_copy(prev, acc, i_sem.at[0])
        fill.start()
        fill.wait()
    for r in range(n):
        weight_copy(r).wait()

    def step(f, carry):
        slot = lax.rem(f, 2)

        @pl.when(f + 1 < fc)
        def _():
            token_copies(f + 1, 1 - slot, start)

        token_copies(f, slot, wait)
        xh, xl = split(jnp.concatenate([xb[slot, k] for k in range(kb)], axis=1))
        ch, cl = split(jnp.concatenate([cb[slot, k] for k in range(kb)], axis=1))
        uh, ul = split(w[0, f].reshape(kb * blk, blk))
        dh, dl = split(jnp.concatenate([w[1, f, k] for k in range(kb)], axis=1))

        wide = dot(xh, jnp.concatenate([uh, ul], axis=1), NN)
        pre = wide[:, :blk] + (wide[:, blk:] + dot(xl, uh, NN))
        wide = dot(ch, jnp.concatenate([dh, dl], axis=0), NT)
        grad_act = wide[:, :blk] + (wide[:, blk:] + dot(cl, dh, NT))
        sig = jax.nn.sigmoid(pre)
        act = pre * sig
        grad_pre = grad_act * sig * (1.0 + pre * (1.0 - sig))

        ah, al = split(act.T)
        tall = dot(jnp.concatenate([ah, al], axis=0), ch, NN)
        grad_down = tall[:blk] + (tall[blk:] + dot(ah, cl, NN))
        gh, gl = split(grad_pre.T)
        tall = dot(jnp.concatenate([gh, gl], axis=0), xh, NN)
        grad_up = tall[:blk] + (tall[blk:] + dot(gh, xl, NN))
        ph, plow = split(grad_pre)
        back = dot(jnp.concatenate([ph, plow], axis=1), jnp.concatenate([uh, uh], axis=1), NT)
        back = back + dot(ph, ul, NT)
        for k in range(kb):
            part = slice(k * blk, (k + 1) * blk)
            w[0, f, k] = grad_up[:, part].T
            w[1, f, k] = grad_down[:, part]
            at = up_at[f * kb + k]
            acc[at] = acc[at] + back[:, part]
        return carry

    lax.fori_loop(0, fc, step, 0)
    grad_copies(start)
    if last:
        copies = []
        for r in range(heads):
            for j in range(span):
                for side in range(2):
                    copies.append(pltpu.make_async_copy(
                        acc.at[(hid ^ r) * span + j, pl.ds(side * rows, rows)],
                        outs[2 * side + r % 2].at[r // 2, :, pl.ds(j * blk, blk)],
                        i_sem.at[len(copies)]))
    else:
        copies = [pltpu.make_async_copy(acc, outs[0], i_sem.at[0])]
    for copy in copies:
        copy.start()
    for copy in copies:
        copy.wait()
    grad_copies(wait)


def block_pass(x, cot, got, slabs, up_at, down_at, me, hid, tok, heads, prev, sizes, last, awaits, loose):
    fc = up_at.shape[0]
    n = len(slabs)
    starts, parts = zip(*slabs)
    kb, q, blk = parts[0].shape[2:]
    rows, width = x.shape
    nb = width // blk
    first = prev is None
    cfg = (starts, sizes, kb, blk, rows, nb, n, q, heads, first, last, len(awaits))
    groups = min(n, 2)
    out = [jax.ShapeDtypeStruct((n // groups, 2, size, kb, q, blk), F32)
           for size in sizes for _ in range(groups)]
    if last:
        out += [jax.ShapeDtypeStruct((heads // 2, rows, width // heads), F32)] * 4
    else:
        out.append(pltpu.HBM((nb, 2 * rows, blk), F32))
    def fixed(*arrays):
        return [pltpu.with_memory_space_constraint(a, pltpu.HBM) for a in arrays]

    parts = [part if loose[r] else fixed(part)[0] for r, part in enumerate(parts)]
    got = [a if r % 2 and r > 1 else fixed(a)[0] for r, a in enumerate(got)]
    operands = fixed(x, cot) + got + parts + ([] if first else fixed(prev)) + awaits
    anywhere = pl.BlockSpec(memory_space=pl.ANY)
    products = 2 * rows * fc * kb * blk * blk
    results = pl.pallas_call(
        functools.partial(kernel, cfg),
        out_shape=out,
        grid_spec=pltpu.PrefetchScalarGridSpec(
            num_scalar_prefetch=3,
            grid=(1,),
            in_specs=[anywhere] * len(operands),
            out_specs=[anywhere] * len(out),
            scratch_shapes=[
                pltpu.VMEM((2, fc, kb, blk, blk), F32),
                pltpu.VMEM((2, kb, 2 * rows, blk), F32),
                pltpu.VMEM((2, kb, 2 * rows, blk), F32),
                pltpu.VMEM((nb, 2 * rows, blk), F32),
                pltpu.SemaphoreType.DMA((n,)),
                pltpu.SemaphoreType.DMA((len(sizes), n)),
                pltpu.SemaphoreType.DMA((2, 4 * kb)),
                pltpu.SemaphoreType.DMA((2 * nb,)),
            ],
        ),
        compiler_params=pltpu.CompilerParams(vmem_limit_bytes=13 * 2**20),
        cost_estimate=pl.CostEstimate(
            flops=8 * 5 * 3 * products, bytes_accessed=16 * 2**20, transcendentals=0),
    )(up_at.reshape(-1), down_at.reshape(-1), jnp.stack([me, hid]), *operands)
    grads = []
    for p, size in enumerate(sizes):
        pair = results[p * groups:(p + 1) * groups]
        if n == 1:
            whole = pair[0].reshape(2, size, kb, tok, q // tok, blk)
            whole = jnp.take(jnp.moveaxis(whole, 3, 0), me ^ jnp.arange(tok), axis=0)
            whole = whole.reshape((tok // 2, 2) + whole.shape[1:])
            pair = whole[:, 0], whole[:, 1]
        grads.append(pair)
    return grads, results[len(sizes) * groups:]


def after(value, *others):
    return lax.optimization_barrier((value, *others))[0]


def shards(inputs, cotangent, up_blocks, down_blocks, up_index, down_index, mom_up, mom_down):
    rows, width = inputs.shape
    blocks, kb, q, blk = up_blocks.shape
    tok, heads = lax.axis_size("tok"), lax.axis_size("hid")
    me, hid = lax.axis_index("tok"), lax.axis_index("hid")
    inner = inner_size(tok)
    pair = inner
    near = bits_below(inner)
    far = [b for b in range(0, tok, 2 * inner)]
    half = blocks // 2
    cuts = [round(half * part / 14) for part in (0, 3, 7, 11, 14)]
    edges = [0, cuts[2], half]
    calls = [cuts[:2], cuts[1:3], cuts[2:]]
    side = (me // pair) % 2
    scale = (rows * tok) ** (-0.5)
    span = width // heads

    def weights(which, f0, f1):
        at = which * half + f0
        return jnp.stack([
            lax.dynamic_slice(a, (at, 0, 0, 0), (f1 - f0, kb, q, blk))
            for a in (up_blocks, down_blocks)])

    both = jnp.stack([
        lax.dynamic_slice(a, (0, hid * span), (rows, span)) for a in (inputs, cotangent)])
    tokens = swap(both, "tok", pair)
    mine, other = weights(side, 0, half), weights(1 - side, 0, half)
    most = far[-1] | pair
    parts = {0: [(0, mine)], most: [(0, swap(other, "tok", most))]}
    for bit in near:
        for r in list(parts):
            parts[r | bit] = [(0, swap(parts[r][0][1], "tok", bit))]

    pieces = {0: after(tokens, parts[most][0][1], parts[1][0][1])}
    for bit in reversed(bits_below(heads)[1:]):
        for r in list(pieces):
            pieces[r | bit] = swap(pieces[r], "hid", bit)
    pieces[1] = swap(pieces[0], "hid", 1)

    sends = [(1 - side, pair)] + [
        send for r in far if r for send in ((side, r), (1 - side, r | pair)) if send[1] != most]
    for which, to in sends:
        for r in [to] + [to | bit for bit in range(1, inner)]:
            parts[r] = []
        for f0, f1 in zip(edges[:-1], edges[1:]):
            source = weights(which, f0, f1)
            if f0:
                source = after(source, parts[to][0][1], pieces[1])
            fresh = {to: swap(source, "tok", to)}
            for bit in near:
                fresh.update({r | bit: swap(part, "tok", bit) for r, part in fresh.items()})
            for r, part in fresh.items():
                parts[r].append((f0, part))
    before = [part for r in parts if r & 1 for f0, part in parts[r] if f0]
    held = [parts[to][0][1] for _, to in sends] + [parts[most | 1][0][1]]
    for r in range(2, heads, 2):
        pieces[r | 1] = swap(after(pieces[r], *held), "hid", 1)
    got = [pieces[r] for r in range(heads)]

    mine = []

    def finish(even, got_back):
        total = even + got_back
        left = [b for b in reversed(bits_below(tok)) if b != 1]
        for bit in near[1:] + [b for b in bits_below(tok) if b > pair]:
            p = left.index(bit)
            left.remove(bit)
            total = total.reshape((2 ** p, 2, -1) + total.shape[1:])
            back = swap(total[:, 1], "tok", bit)
            total = (total[:, 0] + back).reshape((-1,) + total.shape[3:])
        folded.append(back)
        mine.append(total)

    partial = None
    crossed, folded = [], []
    kept = None
    for call in calls:
        f0, f1 = call[0], call[-1]
        slabs = []
        for r in range(tok):
            start, part = [(start, part) for start, part in parts[r] if start <= f0][-1]
            slabs.append((f0 - start, part))
        if q % 8:
            whole = jnp.stack([part[:, at:at + f1 - f0] for at, part in slabs])
            whole = jnp.take(whole, me ^ jnp.arange(tok), axis=0)
            slabs = [(0, jnp.moveaxis(whole, 0, 3).reshape(2, f1 - f0, kb, blk, blk))]
        at = (side * half + f0, 0)
        grads, rest = block_pass(
            inputs, cotangent, got, slabs,
            lax.dynamic_slice(up_index, at, (f1 - f0, kb)),
            lax.dynamic_slice(down_index, at, (f1 - f0, kb)),
            me, hid, tok, heads, partial,
            [b - a for a, b in zip(call[:-1], call[1:])], f1 == half,
            crossed[:1] if f1 == half else [],
            [f1 < half and r & 1 and len(parts[r]) > 1 for r in range(tok)])
        partial = rest[0]
        if kept:
            finish(kept[0], after(kept[1], partial))
            kept = None

        for even, odd in grads:
            got_back = swap(after(odd, *before, *folded[-2:-1]), "tok", 1)
            before = [got_back]
            crossed.append(got_back)
            if len(crossed) == 2:
                kept = even, got_back
                continue
            finish(even, got_back)
    shares = []
    for side_rows in range(2):
        even, odd = rest[2 * side_rows:2 * side_rows + 2]
        total = even + after(swap(odd, "hid", 1), crossed[1])
        for bit in bits_below(heads)[1:]:
            total = total.reshape((total.shape[0] // 2, 2) + total.shape[1:])
            total = total[:, 0] + swap(total[:, 1], "hid", bit)
        shares.append(total[0])
    input_grad = shares[0] + swap(shares[1], "tok", pair)

    other = [swap(after(total[1], *crossed[p + 1:p + 2]), "tok", pair) for p, total in enumerate(mine)]
    mine = jnp.concatenate([total[0] for total in mine], axis=1)
    other = jnp.concatenate(other, axis=1)
    ordered = jnp.concatenate(
        [jnp.where(side == 0, mine, other), jnp.where(side == 0, other, mine)], axis=1)
    return (
        input_grad,
        0.9 * mom_up + scale * ordered[0],
        0.9 * mom_down + scale * ordered[1],
    )


def solution(mesh):
    return jax.shard_map(
        shards,
        mesh=mesh,
        in_specs=(
            P("tok", None),
            P("tok", None),
            P("hid", None, "tok", None),
            P("hid", None, "tok", None),
            P("hid", None),
            P("hid", None),
            P("hid", None, "tok", None),
            P("hid", None, "tok", None),
        ),
        out_specs=(P("tok", "hid"), P("hid", None, "tok", None), P("hid", None, "tok", None)),
        check_vma=False,
    )
```

```python
import functools

import jax
import jax.numpy as jnp
from jax import lax
from jax.experimental import pallas as pl
from jax.experimental.pallas import tpu as pltpu
from jax.sharding import PartitionSpec as P

F32, BF16 = jnp.float32, jnp.bfloat16
NN = (((1,), (0,)), ((), ()))
NT = (((1,), (1,)), ((), ()))


def swap(value, axis, bit):
    size = lax.axis_size(axis)
    return lax.ppermute(value, axis, [(i, i ^ bit) for i in range(size)])


def bits_below(size):
    return [1 << i for i in range(size.bit_length() - 1)]


def inner_size(size):
    inner = 1
    while inner * inner * 8 <= size:
        inner *= 2
    return inner


def split(value):
    high = value.astype(BF16)
    return high, (value - high.astype(F32)).astype(BF16)


def dot(a, b, dims):
    return lax.dot_general(a, b, dims, preferred_element_type=F32)


def kernel(cfg, up_at, down_at, place, *refs):
    starts, sizes, kb, blk, rows, nb, n, q, heads, first, last, awaits = cfg
    fc = sum(sizes)
    refs = list(refs)
    groups = min(n, 2)
    x_own, c_own = refs[:2]
    got, refs = refs[2:2 + heads], refs[2 + heads:]
    slabs, refs = refs[:n], refs[n:]
    prev = None
    if not first:
        prev, refs = refs[0], refs[1:]
    refs = refs[awaits:]
    grads = []
    for _ in sizes:
        grads.append(refs[:groups])
        refs = refs[groups:]
    outs, refs = refs[:4 if last else 1], refs[4 if last else 1:]
    w, xb, cb, acc, w_sem, g_sem, x_sem, i_sem = refs
    me, hid = place[0], place[1]
    span = nb // heads

    def weight_copy(r):
        start = pl.multiple_of((me ^ r) * q, q) if n > 1 else 0
        return pltpu.make_async_copy(
            slabs[r].at[:, pl.ds(starts[r], fc)], w.at[:, :, :, pl.ds(start, q), :], w_sem.at[r])

    def grad_copies(act):
        for r in range(n):
            start = pl.multiple_of((me ^ r) * q, q) if n > 1 else 0
            f0 = 0
            for p, size in enumerate(sizes):
                act(pltpu.make_async_copy(
                    w.at[:, pl.ds(f0, size), :, pl.ds(start, q), :],
                    grads[p][r % 2].at[r // 2], g_sem.at[p, r]))
                f0 += size

    def token_copies(f, slot, act):
        for k in range(kb):
            for i, (own, ats, buf) in enumerate(((x_own, up_at, xb), (c_own, down_at, cb))):
                at = ats[f * kb + k]
                col = pl.multiple_of(at * blk, blk)
                act(pltpu.make_async_copy(
                    own.at[:, pl.ds(col, blk)], buf.at[slot, k, pl.ds(0, rows)],
                    x_sem.at[slot, 4 * k + 2 * i]))
                col = pl.multiple_of(lax.rem(at, span) * blk, blk)
                holder = lax.div(at, span) ^ hid
                for r in range(heads):
                    @pl.when(holder == r)
                    def _():
                        act(pltpu.make_async_copy(
                            got[r].at[i, :, pl.ds(col, blk)],
                            buf.at[slot, k, pl.ds(rows, rows)],
                            x_sem.at[slot, 4 * k + 2 * i + 1]))

    def start(copy):
        copy.start()

    def wait(copy):
        copy.wait()

    for r in range(n):
        weight_copy(r).start()
    token_copies(0, 0, start)
    if first:
        acc[...] = jnp.zeros_like(acc)
    else:
        fill = pltpu.make_async_copy(prev, acc, i_sem.at[0])
        fill.start()
        fill.wait()
    for r in range(n):
        weight_copy(r).wait()

    def step(f, carry):
        slot = lax.rem(f, 2)

        @pl.when(f + 1 < fc)
        def _():
            token_copies(f + 1, 1 - slot, start)

        token_copies(f, slot, wait)
        xh, xl = split(jnp.concatenate([xb[slot, k] for k in range(kb)], axis=1))
        ch, cl = split(jnp.concatenate([cb[slot, k] for k in range(kb)], axis=1))
        uh, ul = split(w[0, f].reshape(kb * blk, blk))
        dh, dl = split(jnp.concatenate([w[1, f, k] for k in range(kb)], axis=1))

        wide = dot(xh, jnp.concatenate([uh, ul], axis=1), NN)
        pre = wide[:, :blk] + (wide[:, blk:] + dot(xl, uh, NN))
        wide = dot(ch, jnp.concatenate([dh, dl], axis=0), NT)
        grad_act = wide[:, :blk] + (wide[:, blk:] + dot(cl, dh, NT))
        sig = jax.nn.sigmoid(pre)
        act = pre * sig
        grad_pre = grad_act * sig * (1.0 + pre * (1.0 - sig))

        ah, al = split(act.T)
        tall = dot(jnp.concatenate([ah, al], axis=0), ch, NN)
        grad_down = tall[:blk] + (tall[blk:] + dot(ah, cl, NN))
        gh, gl = split(grad_pre.T)
        tall = dot(jnp.concatenate([gh, gl], axis=0), xh, NN)
        grad_up = tall[:blk] + (tall[blk:] + dot(gh, xl, NN))
        ph, plow = split(grad_pre)
        back = dot(jnp.concatenate([ph, plow], axis=1), jnp.concatenate([uh, uh], axis=1), NT)
        back = back + dot(ph, ul, NT)
        for k in range(kb):
            part = slice(k * blk, (k + 1) * blk)
            w[0, f, k] = grad_up[:, part].T
            w[1, f, k] = grad_down[:, part]
            at = up_at[f * kb + k]
            acc[at] = acc[at] + back[:, part]
        return carry

    lax.fori_loop(0, fc, step, 0)
    grad_copies(start)
    if last:
        copies = []
        for r in range(heads):
            for j in range(span):
                for side in range(2):
                    copies.append(pltpu.make_async_copy(
                        acc.at[(hid ^ r) * span + j, pl.ds(side * rows, rows)],
                        outs[2 * side + r % 2].at[r // 2, :, pl.ds(j * blk, blk)],
                        i_sem.at[len(copies)]))
    else:
        copies = [pltpu.make_async_copy(acc, outs[0], i_sem.at[0])]
    for copy in copies:
        copy.start()
    for copy in copies:
        copy.wait()
    grad_copies(wait)


def block_pass(x, cot, got, slabs, up_at, down_at, me, hid, tok, heads, prev, sizes, last, awaits, loose):
    fc = up_at.shape[0]
    n = len(slabs)
    starts, parts = zip(*slabs)
    kb, q, blk = parts[0].shape[2:]
    rows, width = x.shape
    nb = width // blk
    first = prev is None
    cfg = (starts, sizes, kb, blk, rows, nb, n, q, heads, first, last, len(awaits))
    groups = min(n, 2)
    out = [jax.ShapeDtypeStruct((n // groups, 2, size, kb, q, blk), F32)
           for size in sizes for _ in range(groups)]
    if last:
        out += [jax.ShapeDtypeStruct((heads // 2, rows, width // heads), F32)] * 4
    else:
        out.append(pltpu.HBM((nb, 2 * rows, blk), F32))
    def fixed(*arrays):
        return [pltpu.with_memory_space_constraint(a, pltpu.HBM) for a in arrays]

    parts = [part if loose[r] else fixed(part)[0] for r, part in enumerate(parts)]
    got = [a if r % 2 and r > 1 else fixed(a)[0] for r, a in enumerate(got)]
    operands = fixed(x, cot) + got + parts + ([] if first else fixed(prev)) + awaits
    anywhere = pl.BlockSpec(memory_space=pl.ANY)
    products = 2 * rows * fc * kb * blk * blk
    results = pl.pallas_call(
        functools.partial(kernel, cfg),
        out_shape=out,
        grid_spec=pltpu.PrefetchScalarGridSpec(
            num_scalar_prefetch=3,
            grid=(1,),
            in_specs=[anywhere] * len(operands),
            out_specs=[anywhere] * len(out),
            scratch_shapes=[
                pltpu.VMEM((2, fc, kb, blk, blk), F32),
                pltpu.VMEM((2, kb, 2 * rows, blk), F32),
                pltpu.VMEM((2, kb, 2 * rows, blk), F32),
                pltpu.VMEM((nb, 2 * rows, blk), F32),
                pltpu.SemaphoreType.DMA((n,)),
                pltpu.SemaphoreType.DMA((len(sizes), n)),
                pltpu.SemaphoreType.DMA((2, 4 * kb)),
                pltpu.SemaphoreType.DMA((2 * nb,)),
            ],
        ),
        compiler_params=pltpu.CompilerParams(vmem_limit_bytes=13 * 2**20),
        cost_estimate=pl.CostEstimate(
            flops=8 * 5 * 3 * products, bytes_accessed=16 * 2**20, transcendentals=0),
    )(up_at.reshape(-1), down_at.reshape(-1), jnp.stack([me, hid]), *operands)
    grads = []
    for p, size in enumerate(sizes):
        pair = results[p * groups:(p + 1) * groups]
        if n == 1:
            whole = pair[0].reshape(2, size, kb, tok, q // tok, blk)
            whole = jnp.take(jnp.moveaxis(whole, 3, 0), me ^ jnp.arange(tok), axis=0)
            whole = whole.reshape((tok // 2, 2) + whole.shape[1:])
            pair = whole[:, 0], whole[:, 1]
        grads.append(pair)
    return grads, results[len(sizes) * groups:]


def after(value, *others):
    return lax.optimization_barrier((value, *others))[0]


def shards(inputs, cotangent, up_blocks, down_blocks, up_index, down_index, mom_up, mom_down):
    rows, width = inputs.shape
    blocks, kb, q, blk = up_blocks.shape
    tok, heads = lax.axis_size("tok"), lax.axis_size("hid")
    me, hid = lax.axis_index("tok"), lax.axis_index("hid")
    inner = inner_size(tok)
    pair = inner
    near = bits_below(inner)
    far = [b for b in range(0, tok, 2 * inner)]
    half = blocks // 2
    cuts = [round(half * part / 14) for part in (0, 3, 7, 11, 14)]
    edges = [0, cuts[2], half]
    calls = [cuts[:2], cuts[1:3], cuts[2:]]
    side = (me // pair) % 2
    scale = (rows * tok) ** (-0.5)
    span = width // heads

    def weights(which, f0, f1):
        at = which * half + f0
        return jnp.stack([
            lax.dynamic_slice(a, (at, 0, 0, 0), (f1 - f0, kb, q, blk))
            for a in (up_blocks, down_blocks)])

    both = jnp.stack([
        lax.dynamic_slice(a, (0, hid * span), (rows, span)) for a in (inputs, cotangent)])
    tokens = swap(both, "tok", pair)
    mine, other = weights(side, 0, half), weights(1 - side, 0, half)
    most = far[-1] | pair
    parts = {0: [(0, mine)], most: [(0, swap(other, "tok", most))]}
    for bit in near:
        for r in list(parts):
            parts[r | bit] = [(0, swap(parts[r][0][1], "tok", bit))]

    pieces = {0: after(tokens, parts[most][0][1], parts[1][0][1])}
    for bit in reversed(bits_below(heads)[1:]):
        for r in list(pieces):
            pieces[r | bit] = swap(pieces[r], "hid", bit)
    pieces[1] = swap(pieces[0], "hid", 1)

    sends = [(1 - side, pair)] + [
        send for r in far if r for send in ((side, r), (1 - side, r | pair)) if send[1] != most]
    for which, to in sends:
        for r in [to] + [to | bit for bit in range(1, inner)]:
            parts[r] = []
        for f0, f1 in zip(edges[:-1], edges[1:]):
            source = weights(which, f0, f1)
            if f0:
                source = after(source, parts[to][0][1], pieces[1])
            fresh = {to: swap(source, "tok", to)}
            for bit in near:
                fresh.update({r | bit: swap(part, "tok", bit) for r, part in fresh.items()})
            for r, part in fresh.items():
                parts[r].append((f0, part))
    before = [part for r in parts if r & 1 for f0, part in parts[r] if f0]
    held = [parts[to][0][1] for _, to in sends] + [parts[most | 1][0][1]]
    for r in range(2, heads, 2):
        pieces[r | 1] = swap(after(pieces[r], *held), "hid", 1)
    got = [pieces[r] for r in range(heads)]

    mine = []

    def finish(even, got_back):
        total = even + got_back
        left = [b for b in reversed(bits_below(tok)) if b != 1]
        for bit in near[1:] + [b for b in bits_below(tok) if b > pair]:
            p = left.index(bit)
            left.remove(bit)
            total = total.reshape((2 ** p, 2, -1) + total.shape[1:])
            back = swap(total[:, 1], "tok", bit)
            total = (total[:, 0] + back).reshape((-1,) + total.shape[3:])
        folded.append(back)
        mine.append(total)

    partial = None
    crossed, folded = [], []
    kept = None
    for call in calls:
        f0, f1 = call[0], call[-1]
        slabs = []
        for r in range(tok):
            start, part = [(start, part) for start, part in parts[r] if start <= f0][-1]
            slabs.append((f0 - start, part))
        if q % 8:
            whole = jnp.stack([part[:, at:at + f1 - f0] for at, part in slabs])
            whole = jnp.take(whole, me ^ jnp.arange(tok), axis=0)
            slabs = [(0, jnp.moveaxis(whole, 0, 3).reshape(2, f1 - f0, kb, blk, blk))]
        at = (side * half + f0, 0)
        grads, rest = block_pass(
            inputs, cotangent, got, slabs,
            lax.dynamic_slice(up_index, at, (f1 - f0, kb)),
            lax.dynamic_slice(down_index, at, (f1 - f0, kb)),
            me, hid, tok, heads, partial,
            [b - a for a, b in zip(call[:-1], call[1:])], f1 == half,
            crossed[:1] if f1 == half else [],
            [f1 < half and r & 1 and len(parts[r]) > 1 for r in range(tok)])
        partial = rest[0]
        if kept:
            finish(kept[0], after(kept[1], partial))
            kept = None

        for even, odd in grads:
            if len(crossed) > 2:
                before = crossed[-1:]
            got_back = swap(after(odd, *before), "tok", 1)
            before = []
            crossed.append(got_back)
            if len(crossed) == 2:
                kept = even, got_back
                continue
            finish(even, got_back)
    shares = []
    for side_rows in range(2):
        even, odd = rest[2 * side_rows:2 * side_rows + 2]
        total = even + after(swap(odd, "hid", 1), crossed[1])
        for bit in bits_below(heads)[1:]:
            total = total.reshape((total.shape[0] // 2, 2) + total.shape[1:])
            total = total[:, 0] + swap(total[:, 1], "hid", bit)
        shares.append(total[0])
    input_grad = shares[0] + swap(shares[1], "tok", pair)

    other = [swap(after(total[1], *crossed[p + 1:p + 2]), "tok", pair) for p, total in enumerate(mine)]
    mine = jnp.concatenate([total[0] for total in mine], axis=1)
    other = jnp.concatenate(other, axis=1)
    ordered = jnp.concatenate(
        [jnp.where(side == 0, mine, other), jnp.where(side == 0, other, mine)], axis=1)
    return (
        input_grad,
        0.9 * mom_up + scale * ordered[0],
        0.9 * mom_down + scale * ordered[1],
    )


def solution(mesh):
    return jax.shard_map(
        shards,
        mesh=mesh,
        in_specs=(
            P("tok", None),
            P("tok", None),
            P("hid", None, "tok", None),
            P("hid", None, "tok", None),
            P("hid", None),
            P("hid", None),
            P("hid", None, "tok", None),
            P("hid", None, "tok", None),
        ),
        out_specs=(P("tok", "hid"), P("hid", None, "tok", None), P("hid", None, "tok", None)),
        check_vma=False,
    )
```

```python
import functools

import jax
import jax.numpy as jnp
from jax import lax
from jax.experimental import pallas as pl
from jax.experimental.pallas import tpu as pltpu
from jax.sharding import PartitionSpec as P

F32, BF16 = jnp.float32, jnp.bfloat16
NN = (((1,), (0,)), ((), ()))
NT = (((1,), (1,)), ((), ()))


def swap(value, axis, bit):
    size = lax.axis_size(axis)
    return lax.ppermute(value, axis, [(i, i ^ bit) for i in range(size)])


def bits_below(size):
    return [1 << i for i in range(size.bit_length() - 1)]


def inner_size(size):
    inner = 1
    while inner * inner * 8 <= size:
        inner *= 2
    return inner


def split(value):
    high = value.astype(BF16)
    return high, (value - high.astype(F32)).astype(BF16)


def dot(a, b, dims):
    return lax.dot_general(a, b, dims, preferred_element_type=F32)


def kernel(cfg, up_at, down_at, place, *refs):
    starts, sizes, kb, blk, rows, nb, n, q, heads, first, last, awaits = cfg
    fc = sum(sizes)
    refs = list(refs)
    groups = min(n, 2)
    x_own, c_own = refs[:2]
    got, refs = refs[2:2 + 3 * heads], refs[2 + 3 * heads:]
    slabs, refs = refs[:n], refs[n:]
    prev = None
    if not first:
        prev, refs = refs[0], refs[1:]
    refs = refs[awaits:]
    grads = []
    for _ in sizes:
        grads.append(refs[:groups])
        refs = refs[groups:]
    outs, refs = refs[:4 if last else 1], refs[4 if last else 1:]
    w, xb, cb, acc, w_sem, g_sem, x_sem, i_sem = refs
    me, hid = place[0], place[1]
    span = nb // heads

    def weight_copy(r):
        start = pl.multiple_of((me ^ r) * q, q) if n > 1 else 0
        return pltpu.make_async_copy(
            slabs[r].at[:, pl.ds(starts[r], fc)], w.at[:, :, :, pl.ds(start, q), :], w_sem.at[r])

    def grad_copies(act):
        for r in range(n):
            start = pl.multiple_of((me ^ r) * q, q) if n > 1 else 0
            f0 = 0
            for p, size in enumerate(sizes):
                act(pltpu.make_async_copy(
                    w.at[:, pl.ds(f0, size), :, pl.ds(start, q), :],
                    grads[p][r * groups // n].at[r % (n // groups)], g_sem.at[p, r]))
                f0 += size

    def token_copies(f, slot, act):
        for k in range(kb):
            for i, (own, ats, buf) in enumerate(((x_own, up_at, xb), (c_own, down_at, cb))):
                at = ats[f * kb + k]
                col = pl.multiple_of(at * blk, blk)
                act(pltpu.make_async_copy(
                    own.at[:, pl.ds(col, blk)], buf.at[slot, k, pl.ds(0, rows)],
                    x_sem.at[slot, i, k, 0]))
                col = pl.multiple_of(lax.rem(at, span) * blk, blk)
                holder = lax.div(at, span) ^ hid
                for r in range(heads):
                    @pl.when(holder == r)
                    def _():
                        for group in range(1, 4):
                            act(pltpu.make_async_copy(
                                got[(group - 1) * heads + r].at[i, :, pl.ds(col, blk)],
                                buf.at[slot, k, pl.ds(group * rows, rows)],
                                x_sem.at[slot, i, k, group]))

    def start(copy):
        copy.start()

    def wait(copy):
        copy.wait()

    for r in range(n):
        weight_copy(r).start()
    token_copies(0, 0, start)
    if first:
        acc[...] = jnp.zeros_like(acc)
    else:
        fill = pltpu.make_async_copy(prev, acc, i_sem.at[0])
        fill.start()
        fill.wait()
    for r in range(n):
        weight_copy(r).wait()

    def step(f, carry):
        slot = lax.rem(f, 2)

        @pl.when(f + 1 < fc)
        def _():
            token_copies(f + 1, 1 - slot, start)

        token_copies(f, slot, wait)
        xh, xl = split(jnp.concatenate([xb[slot, k] for k in range(kb)], axis=1))
        ch, cl = split(jnp.concatenate([cb[slot, k] for k in range(kb)], axis=1))
        uh, ul = split(w[0, f].reshape(kb * blk, blk))
        dh, dl = split(jnp.concatenate([w[1, f, k] for k in range(kb)], axis=1))

        wide = dot(xh, jnp.concatenate([uh, ul], axis=1), NN)
        pre = wide[:, :blk] + (wide[:, blk:] + dot(xl, uh, NN))
        wide = dot(ch, jnp.concatenate([dh, dl], axis=0), NT)
        grad_act = wide[:, :blk] + (wide[:, blk:] + dot(cl, dh, NT))
        sig = jax.nn.sigmoid(pre)
        act = pre * sig
        grad_pre = grad_act * sig * (1.0 + pre * (1.0 - sig))

        ah, al = split(act.T)
        tall = dot(jnp.concatenate([ah, al], axis=0), ch, NN)
        grad_down = tall[:blk] + (tall[blk:] + dot(ah, cl, NN))
        gh, gl = split(grad_pre.T)
        tall = dot(jnp.concatenate([gh, gl], axis=0), xh, NN)
        grad_up = tall[:blk] + (tall[blk:] + dot(gh, xl, NN))
        ph, plow = split(grad_pre)
        back = dot(jnp.concatenate([ph, plow], axis=1), jnp.concatenate([uh, uh], axis=1), NT)
        back = back + dot(ph, ul, NT)
        for k in range(kb):
            part = slice(k * blk, (k + 1) * blk)
            w[0, f, k] = grad_up[:, part].T
            w[1, f, k] = grad_down[:, part]
            at = up_at[f * kb + k]
            acc[at] = acc[at] + back[:, part]
        return carry

    lax.fori_loop(0, fc, step, 0)
    grad_copies(start)
    if last:
        copies = []
        for r in range(heads):
            for j in range(span):
                for group in range(4):
                    copies.append(pltpu.make_async_copy(
                        acc.at[(hid ^ r) * span + j, pl.ds(group * rows, rows)],
                        outs[2 * (group % 2) + r % 2].at[
                            r // 2, group // 2, :, pl.ds(j * blk, blk)],
                        i_sem.at[len(copies)]))
    else:
        copies = [pltpu.make_async_copy(acc, outs[0], i_sem.at[0])]
    for copy in copies:
        copy.start()
    for copy in copies:
        copy.wait()
    grad_copies(wait)


def block_pass(x, cot, got, slabs, up_at, down_at, me, hid, tok, heads, prev, sizes, last, awaits, loose):
    fc = up_at.shape[0]
    n = len(slabs)
    starts, parts = zip(*slabs)
    kb, q, blk = parts[0].shape[2:]
    rows, width = x.shape
    nb = width // blk
    first = prev is None
    cfg = (starts, sizes, kb, blk, rows, nb, n, q, heads, first, last, len(awaits))
    groups = min(n, 2)
    out = [jax.ShapeDtypeStruct((n // groups, 2, size, kb, q, blk), F32)
           for size in sizes for _ in range(groups)]
    if last:
        out += [jax.ShapeDtypeStruct((heads // 2, 2, rows, width // heads), F32)] * 4
    else:
        out.append(pltpu.HBM((nb, 4 * rows, blk), F32))
    def fixed(*arrays):
        return [pltpu.with_memory_space_constraint(a, pltpu.HBM) for a in arrays]

    parts = [part if loose[r] else fixed(part)[0] for r, part in enumerate(parts)]
    late = {2 * heads - 1, 3 * heads - 2, 3 * heads - 1}
    got = [a if r in late else fixed(a)[0] for r, a in enumerate(got)]
    operands = fixed(x, cot) + got + parts + ([] if first else fixed(prev)) + awaits
    anywhere = pl.BlockSpec(memory_space=pl.ANY)
    products = 4 * rows * fc * kb * blk * blk
    results = pl.pallas_call(
        functools.partial(kernel, cfg),
        out_shape=out,
        grid_spec=pltpu.PrefetchScalarGridSpec(
            num_scalar_prefetch=3,
            grid=(1,),
            in_specs=[anywhere] * len(operands),
            out_specs=[anywhere] * len(out),
            scratch_shapes=[
                pltpu.VMEM((2, fc, kb, blk, blk), F32),
                pltpu.VMEM((2, kb, 4 * rows, blk), F32),
                pltpu.VMEM((2, kb, 4 * rows, blk), F32),
                pltpu.VMEM((nb, 4 * rows, blk), F32),
                pltpu.SemaphoreType.DMA((n,)),
                pltpu.SemaphoreType.DMA((len(sizes), n)),
                pltpu.SemaphoreType.DMA((2, 2, kb, 4)),
                pltpu.SemaphoreType.DMA((4 * nb,)),
            ],
        ),
        compiler_params=pltpu.CompilerParams(vmem_limit_bytes=24 * 2**20),
        cost_estimate=pl.CostEstimate(
            flops=8 * 5 * 3 * products, bytes_accessed=16 * 2**20, transcendentals=0),
    )(up_at.reshape(-1), down_at.reshape(-1), jnp.stack([me, hid]), *operands)
    grads = []
    for p, size in enumerate(sizes):
        pair = results[p * groups:(p + 1) * groups]
        if n == 1:
            whole = pair[0].reshape(2, size, kb, tok, q // tok, blk)
            whole = jnp.take(jnp.moveaxis(whole, 3, 0), me ^ jnp.arange(tok), axis=0)
            whole = whole.reshape((2, tok // 2) + whole.shape[1:])
            pair = whole[0], whole[1]
        grads.append(pair)
    return grads, results[len(sizes) * groups:]


def after(value, *others):
    return lax.optimization_barrier((value, *others))[0]


def shards(inputs, cotangent, up_blocks, down_blocks, up_index, down_index, mom_up, mom_down):
    rows, width = inputs.shape
    blocks, kb, q, blk = up_blocks.shape
    tok, heads = lax.axis_size("tok"), lax.axis_size("hid")
    me, hid = lax.axis_index("tok"), lax.axis_index("hid")
    pair = inner_size(tok)
    most = [b for b in bits_below(tok) if b not in (1, pair)]
    quarter = -(-blocks // 4)
    if quarter * 4 != blocks:
        extra = 4 * quarter - blocks
        up_blocks, down_blocks = (
            jnp.pad(a, ((0, extra), (0, 0), (0, 0), (0, 0))) for a in (up_blocks, down_blocks))
        up_index, down_index = (jnp.pad(a, ((0, extra), (0, 0))) for a in (up_index, down_index))
    cuts = [round(quarter * part / 7) for part in (0, 2, 5, 7)]
    calls = [cuts[:2], cuts[1:]]
    mine = (me // pair) % 2 * 2 + me % 2
    scale = (rows * tok) ** (-0.5)
    span = width // heads

    def weights(which):
        at = which * quarter
        return [lax.dynamic_slice(a, (at, 0, 0, 0), (quarter, kb, q, blk))
                for a in (up_blocks, down_blocks)]

    both = jnp.stack([
        lax.dynamic_slice(a, (0, hid * span), (rows, span)) for a in (inputs, cotangent)])
    x_tokens = swap(both, "tok", 1)
    z_tokens = swap(both, "tok", pair)

    keep = {0: jnp.stack(weights(mine)), pair: jnp.stack(weights(mine ^ 2))}
    give = jnp.stack([jnp.stack(weights(mine ^ 1)), jnp.stack(weights(mine ^ 3))])
    masks = [sum(b for i, b in enumerate(most) if j >> i & 1) for j in range(2 ** len(most))]
    far = [m | p for m in reversed(masks) if m for p in (pair, 0)]

    parts = {0: keep[0]}
    waits = []
    for to in far:
        parts[to] = swap(after(keep[to & pair], *waits), "tok", to)
        waits = [parts[to]]
    given = swap(after(give, x_tokens), "tok", 1)
    parts[1] = given[0]
    second = {0: given[0], pair: given[1]}
    parts[pair] = swap(after(keep[pair], z_tokens), "tok", pair)
    for to in far:
        parts[to | 1] = swap(after(second[to & pair], *waits), "tok", to)
        waits = [parts[to | 1]]
    parts[pair | 1] = swap(after(second[pair], parts[pair]), "tok", pair)

    xz_tokens = swap(after(z_tokens, given), "tok", 1)
    order = [
        (x_tokens, [parts[far[0]]]),
        (z_tokens, [parts[far[-1]]]),
        (xz_tokens, [parts[far[0] | 1], parts[pair]]),
    ]
    got = []
    crossed_y = []
    for fetched, held in order:
        pieces = {0: after(fetched, *held, *crossed_y)}
        for bit in reversed(bits_below(heads)[1:]):
            for r in list(pieces):
                pieces[r | bit] = swap(pieces[r], "hid", bit)
        crossed_y = [pieces[heads - 2]]
        for r in list(pieces):
            pieces[r | 1] = swap(pieces[r], "hid", 1)
        got.append([pieces[r] for r in range(heads)])
    got = got[0] + got[1] + got[2]

    slabs_of = [parts[r] for r in range(tok)]
    total_of, delivered = [], []
    partial, folded = None, []
    for call in calls:
        f0, f1 = call[0], call[-1]
        slabs = [(f0, part) for part in slabs_of]
        if q % 8:
            whole = jnp.stack([part[:, f0:f1] for part in slabs_of])
            whole = jnp.take(whole, me ^ jnp.arange(tok), axis=0)
            slabs = [(0, jnp.moveaxis(whole, 0, 3).reshape(2, f1 - f0, kb, blk, blk))]
        at = (mine * quarter + f0, 0)
        grads, rest = block_pass(
            inputs, cotangent, got, slabs,
            lax.dynamic_slice(up_index, at, (f1 - f0, kb)),
            lax.dynamic_slice(down_index, at, (f1 - f0, kb)),
            me, hid, tok, heads, partial,
            [b - a for a, b in zip(call[:-1], call[1:])], f1 == quarter, [], [True] * tok)
        partial = rest[0]

        for low, high in grads:
            back = swap(after(high, *folded[-1:], *delivered[-1:]), "tok", tok // 2)
            folded.append(back)
            total = low + back
            left = list(reversed(bits_below(tok)))[1:]
            for bit in reversed(most[:-1]):
                p = left.index(bit)
                left.remove(bit)
                total = total.reshape((2 ** p, 2, -1) + total.shape[1:])
                total = (total[:, 0] + swap(total[:, 1], "tok", bit)).reshape(
                    (-1,) + total.shape[3:])
            total_of.append(total)

    handed = {to: [swap(total[r], "tok", to) if to else total[0] for total in total_of]
              for r, to in enumerate((0, 1, pair, pair | 1))}

    shares, firsts = [], folded[:1]
    for x_side in (1, 0):
        even, odd = rest[2 * x_side:2 * x_side + 2]
        first = swap(after(odd, *firsts), "hid", 1)
        total = even + first
        for bit in bits_below(heads)[1:]:
            total = total.reshape((total.shape[0] // 2, 2) + total.shape[1:])
            total = total[:, 0] + swap(total[:, 1], "hid", bit)
        shares.append(total[0])
    share = shares[1] + swap(shares[0], "tok", 1)
    input_grad = share[0] + swap(share[1], "tok", pair)

    quarters = [jnp.concatenate(rows_of, axis=1) for rows_of in handed.values()]
    for bit in (1, 2):
        flip = mine & bit > 0
        quarters = [jnp.where(flip, quarters[j ^ bit], quarters[j]) for j in range(4)]
    ordered = jnp.concatenate(quarters, axis=1)[:, :blocks]
    return (
        input_grad,
        0.9 * mom_up + scale * ordered[0],
        0.9 * mom_down + scale * ordered[1],
    )


def solution(mesh):
    return jax.shard_map(
        shards,
        mesh=mesh,
        in_specs=(
            P("tok", None),
            P("tok", None),
            P("hid", None, "tok", None),
            P("hid", None, "tok", None),
            P("hid", None),
            P("hid", None),
            P("hid", None, "tok", None),
            P("hid", None, "tok", None),
        ),
        out_specs=(P("tok", "hid"), P("hid", None, "tok", None), P("hid", None, "tok", None)),
        check_vma=False,
    )
```

```python
import functools

import jax
import jax.numpy as jnp
from jax import lax
from jax.experimental import pallas as pl
from jax.experimental.pallas import tpu as pltpu
from jax.sharding import PartitionSpec as P

F32, BF16 = jnp.float32, jnp.bfloat16
NN = (((1,), (0,)), ((), ()))
NT = (((1,), (1,)), ((), ()))


def swap(value, axis, bit):
    size = lax.axis_size(axis)
    return lax.ppermute(value, axis, [(i, i ^ bit) for i in range(size)])


def bits_below(size):
    return [1 << i for i in range(size.bit_length() - 1)]


def inner_size(size):
    inner = 1
    while inner * inner * 8 <= size:
        inner *= 2
    return inner


def split(value):
    high = value.astype(BF16)
    return high, (value - high.astype(F32)).astype(BF16)


def dot(a, b, dims):
    return lax.dot_general(a, b, dims, preferred_element_type=F32)


def kernel(cfg, up_at, down_at, place, *refs):
    starts, sizes, kb, blk, rows, nb, n, q, heads, first, last, awaits = cfg
    fc = sum(sizes)
    refs = list(refs)
    groups = min(n, 2)
    x_own, c_own = refs[:2]
    got, refs = refs[2:2 + 3 * heads], refs[2 + 3 * heads:]
    slabs, refs = refs[:n], refs[n:]
    prev = None
    if not first:
        prev, refs = refs[0], refs[1:]
    refs = refs[awaits:]
    grads = []
    for _ in sizes:
        grads.append(refs[:groups])
        refs = refs[groups:]
    outs, refs = refs[:4 if last else 1], refs[4 if last else 1:]
    w, xb, cb, acc, w_sem, g_sem, x_sem, i_sem = refs
    me, hid = place[0], place[1]
    span = nb // heads

    def weight_copy(r):
        start = pl.multiple_of((me ^ r) * q, q) if n > 1 else 0
        return pltpu.make_async_copy(
            slabs[r].at[:, pl.ds(starts[r], fc)], w.at[:, :, :, pl.ds(start, q), :], w_sem.at[r])

    def grad_copies(act):
        for r in range(n):
            start = pl.multiple_of((me ^ r) * q, q) if n > 1 else 0
            f0 = 0
            for p, size in enumerate(sizes):
                act(pltpu.make_async_copy(
                    w.at[:, pl.ds(f0, size), :, pl.ds(start, q), :],
                    grads[p][r * groups // n].at[r % (n // groups)], g_sem.at[p, r]))
                f0 += size

    def token_copies(f, slot, act):
        for k in range(kb):
            for i, (own, ats, buf) in enumerate(((x_own, up_at, xb), (c_own, down_at, cb))):
                at = ats[f * kb + k]
                col = pl.multiple_of(at * blk, blk)
                act(pltpu.make_async_copy(
                    own.at[:, pl.ds(col, blk)], buf.at[slot, k, pl.ds(0, rows)],
                    x_sem.at[slot, i, k, 0]))
                col = pl.multiple_of(lax.rem(at, span) * blk, blk)
                holder = lax.div(at, span) ^ hid
                for r in range(heads):
                    @pl.when(holder == r)
                    def _():
                        for group in range(1, 4):
                            act(pltpu.make_async_copy(
                                got[(group - 1) * heads + r].at[i, :, pl.ds(col, blk)],
                                buf.at[slot, k, pl.ds(group * rows, rows)],
                                x_sem.at[slot, i, k, group]))

    def start(copy):
        copy.start()

    def wait(copy):
        copy.wait()

    for r in range(n):
        weight_copy(r).start()
    token_copies(0, 0, start)
    if first:
        acc[...] = jnp.zeros_like(acc)
    else:
        fill = pltpu.make_async_copy(prev, acc, i_sem.at[0])
        fill.start()
        fill.wait()
    for r in range(n):
        weight_copy(r).wait()

    def step(f, carry):
        slot = lax.rem(f, 2)

        @pl.when(f + 1 < fc)
        def _():
            token_copies(f + 1, 1 - slot, start)

        token_copies(f, slot, wait)
        xh, xl = split(jnp.concatenate([xb[slot, k] for k in range(kb)], axis=1))
        ch, cl = split(jnp.concatenate([cb[slot, k] for k in range(kb)], axis=1))
        uh, ul = split(w[0, f].reshape(kb * blk, blk))
        dh, dl = split(jnp.concatenate([w[1, f, k] for k in range(kb)], axis=1))

        wide = dot(xh, jnp.concatenate([uh, ul], axis=1), NN)
        pre = wide[:, :blk] + (wide[:, blk:] + dot(xl, uh, NN))
        wide = dot(ch, jnp.concatenate([dh, dl], axis=0), NT)
        grad_act = wide[:, :blk] + (wide[:, blk:] + dot(cl, dh, NT))
        sig = jax.nn.sigmoid(pre)
        act = pre * sig
        grad_pre = grad_act * sig * (1.0 + pre * (1.0 - sig))

        ah, al = split(act.T)
        tall = dot(jnp.concatenate([ah, al], axis=0), ch, NN)
        grad_down = tall[:blk] + (tall[blk:] + dot(ah, cl, NN))
        gh, gl = split(grad_pre.T)
        tall = dot(jnp.concatenate([gh, gl], axis=0), xh, NN)
        grad_up = tall[:blk] + (tall[blk:] + dot(gh, xl, NN))
        ph, plow = split(grad_pre)
        back = dot(jnp.concatenate([ph, plow], axis=1), jnp.concatenate([uh, uh], axis=1), NT)
        back = back + dot(ph, ul, NT)
        for k in range(kb):
            part = slice(k * blk, (k + 1) * blk)
            w[0, f, k] = grad_up[:, part].T
            w[1, f, k] = grad_down[:, part]
            at = up_at[f * kb + k]
            acc[at] = acc[at] + back[:, part]
        return carry

    lax.fori_loop(0, fc, step, 0)
    grad_copies(start)
    if last:
        copies = []
        for r in range(heads):
            for j in range(span):
                for group in range(4):
                    copies.append(pltpu.make_async_copy(
                        acc.at[(hid ^ r) * span + j, pl.ds(group * rows, rows)],
                        outs[2 * (group % 2) + r % 2].at[
                            r // 2, group // 2, :, pl.ds(j * blk, blk)],
                        i_sem.at[len(copies)]))
    else:
        copies = [pltpu.make_async_copy(acc, outs[0], i_sem.at[0])]
    for copy in copies:
        copy.start()
    for copy in copies:
        copy.wait()
    grad_copies(wait)


def block_pass(x, cot, got, slabs, up_at, down_at, me, hid, tok, heads, prev, sizes, last, awaits, loose):
    fc = up_at.shape[0]
    n = len(slabs)
    starts, parts = zip(*slabs)
    kb, q, blk = parts[0].shape[2:]
    rows, width = x.shape
    nb = width // blk
    first = prev is None
    cfg = (starts, sizes, kb, blk, rows, nb, n, q, heads, first, last, len(awaits))
    groups = min(n, 2)
    out = [jax.ShapeDtypeStruct((n // groups, 2, size, kb, q, blk), F32)
           for size in sizes for _ in range(groups)]
    if last:
        out += [jax.ShapeDtypeStruct((heads // 2, 2, rows, width // heads), F32)] * 4
    else:
        out.append(pltpu.HBM((nb, 4 * rows, blk), F32))
    def fixed(*arrays):
        return [pltpu.with_memory_space_constraint(a, pltpu.HBM) for a in arrays]

    parts = [part if loose[r] else fixed(part)[0] for r, part in enumerate(parts)]
    late = {2 * heads - 1, 3 * heads - 2, 3 * heads - 1}
    got = [a if r in late else fixed(a)[0] for r, a in enumerate(got)]
    operands = fixed(x, cot) + got + parts + ([] if first else fixed(prev)) + awaits
    anywhere = pl.BlockSpec(memory_space=pl.ANY)
    products = 4 * rows * fc * kb * blk * blk
    results = pl.pallas_call(
        functools.partial(kernel, cfg),
        out_shape=out,
        grid_spec=pltpu.PrefetchScalarGridSpec(
            num_scalar_prefetch=3,
            grid=(1,),
            in_specs=[anywhere] * len(operands),
            out_specs=[anywhere] * len(out),
            scratch_shapes=[
                pltpu.VMEM((2, fc, kb, blk, blk), F32),
                pltpu.VMEM((2, kb, 4 * rows, blk), F32),
                pltpu.VMEM((2, kb, 4 * rows, blk), F32),
                pltpu.VMEM((nb, 4 * rows, blk), F32),
                pltpu.SemaphoreType.DMA((n,)),
                pltpu.SemaphoreType.DMA((len(sizes), n)),
                pltpu.SemaphoreType.DMA((2, 2, kb, 4)),
                pltpu.SemaphoreType.DMA((4 * nb,)),
            ],
        ),
        compiler_params=pltpu.CompilerParams(vmem_limit_bytes=24 * 2**20),
        cost_estimate=pl.CostEstimate(
            flops=8 * 5 * 3 * products, bytes_accessed=16 * 2**20, transcendentals=0),
    )(up_at.reshape(-1), down_at.reshape(-1), jnp.stack([me, hid]), *operands)
    grads = []
    for p, size in enumerate(sizes):
        pair = results[p * groups:(p + 1) * groups]
        if n == 1:
            whole = pair[0].reshape(2, size, kb, tok, q // tok, blk)
            whole = jnp.take(jnp.moveaxis(whole, 3, 0), me ^ jnp.arange(tok), axis=0)
            whole = whole.reshape((2, tok // 2) + whole.shape[1:])
            pair = whole[0], whole[1]
        grads.append(pair)
    return grads, results[len(sizes) * groups:]


def after(value, *others):
    return lax.optimization_barrier((value, *others))[0]


def shards(inputs, cotangent, up_blocks, down_blocks, up_index, down_index, mom_up, mom_down):
    rows, width = inputs.shape
    blocks, kb, q, blk = up_blocks.shape
    tok, heads = lax.axis_size("tok"), lax.axis_size("hid")
    me, hid = lax.axis_index("tok"), lax.axis_index("hid")
    pair = inner_size(tok)
    most = [b for b in bits_below(tok) if b not in (1, pair)]
    quarter = -(-blocks // 4)
    if quarter * 4 != blocks:
        extra = 4 * quarter - blocks
        up_blocks, down_blocks = (
            jnp.pad(a, ((0, extra), (0, 0), (0, 0), (0, 0))) for a in (up_blocks, down_blocks))
        up_index, down_index = (jnp.pad(a, ((0, extra), (0, 0))) for a in (up_index, down_index))
    cuts = [round(quarter * part / 7) for part in (0, 2, 5, 7)]
    calls = [cuts[:2], cuts[1:]]
    mine = (me // pair) % 2 * 2 + me % 2
    scale = (rows * tok) ** (-0.5)
    span = width // heads

    def weights(which):
        at = which * quarter
        return [lax.dynamic_slice(a, (at, 0, 0, 0), (quarter, kb, q, blk))
                for a in (up_blocks, down_blocks)]

    both = jnp.stack([
        lax.dynamic_slice(a, (0, hid * span), (rows, span)) for a in (inputs, cotangent)])
    x_tokens = swap(both, "tok", 1)
    z_tokens = swap(both, "tok", pair)

    keep = {0: jnp.stack(weights(mine)), pair: jnp.stack(weights(mine ^ 2))}
    give = jnp.stack([jnp.stack(weights(mine ^ 1)), jnp.stack(weights(mine ^ 3))])
    masks = [sum(b for i, b in enumerate(most) if j >> i & 1) for j in range(2 ** len(most))]
    far = [m | p for m in reversed(masks) if m for p in (pair, 0)]

    parts = {0: keep[0]}
    waits = []
    for to in far:
        parts[to] = swap(after(keep[to & pair], *waits), "tok", to)
        waits = [parts[to]]
    given = swap(after(give, x_tokens), "tok", 1)
    parts[1] = given[0]
    second = {0: given[0], pair: given[1]}
    parts[pair] = swap(after(keep[pair], z_tokens), "tok", pair)
    for to in far:
        parts[to | 1] = swap(after(second[to & pair], *waits), "tok", to)
        waits = [parts[to | 1]]
    parts[pair | 1] = swap(after(second[pair], parts[pair]), "tok", pair)

    xz_tokens = swap(after(z_tokens, given), "tok", 1)
    order = [
        (x_tokens, [parts[far[0]]]),
        (z_tokens, [parts[far[-1]]]),
        (xz_tokens, [parts[far[0] | 1], parts[pair]]),
    ]
    got = []
    crossed_y = []
    for fetched, held in order:
        pieces = {0: after(fetched, *held, *crossed_y)}
        for bit in reversed(bits_below(heads)[1:]):
            for r in list(pieces):
                pieces[r | bit] = swap(pieces[r], "hid", bit)
        crossed_y = [pieces[heads - 2]]
        for r in list(pieces):
            pieces[r | 1] = swap(pieces[r], "hid", 1)
        got.append([pieces[r] for r in range(heads)])
    got = got[0] + got[1] + got[2]

    slabs_of = [parts[r] for r in range(tok)]
    partial, made = None, []
    for call in calls:
        f0, f1 = call[0], call[-1]
        slabs = [(f0, part) for part in slabs_of]
        if q % 8:
            whole = jnp.stack([part[:, f0:f1] for part in slabs_of])
            whole = jnp.take(whole, me ^ jnp.arange(tok), axis=0)
            slabs = [(0, jnp.moveaxis(whole, 0, 3).reshape(2, f1 - f0, kb, blk, blk))]
        at = (mine * quarter + f0, 0)
        grads, rest = block_pass(
            inputs, cotangent, got, slabs,
            lax.dynamic_slice(up_index, at, (f1 - f0, kb)),
            lax.dynamic_slice(down_index, at, (f1 - f0, kb)),
            me, hid, tok, heads, partial,
            [b - a for a, b in zip(call[:-1], call[1:])], f1 == quarter, [], [False] * tok)
        partial = rest[0]

        made += grads

    rows_of = [[] for _ in range(4)]
    folded, sent = [], []

    def fold(low, high, *others):
        back = swap(after(high, *folded[-1:], *others), "tok", tok // 2)
        folded.append(back)
        total = low + back
        left = list(reversed(bits_below(tok)))[1:]
        for bit in reversed(most[:-1]):
            p = left.index(bit)
            left.remove(bit)
            total = total.reshape((2 ** p, 2, -1) + total.shape[1:])
            total = (total[:, 0] + swap(total[:, 1], "tok", bit)).reshape((-1,) + total.shape[3:])
        return total

    def hand_over(total, x_waits=(), z_waits=()):
        crossed = swap(after(total[1::2], *sent[-1:], *x_waits), "tok", 1)
        over = swap(after(jnp.stack([total[2], crossed[1]]), *z_waits), "tok", pair)
        sent.append(over)
        for r, got_rows in enumerate((total[0], crossed[0], over[0], over[1])):
            rows_of[r].append(got_rows)

    hand_over(fold(*made[0]))
    second_total = fold(*made[1])

    shares = []
    for x_side in (1, 0):
        even, odd = rest[2 * x_side:2 * x_side + 2]
        total = even + swap(after(odd, folded[0]), "hid", 1)
        for bit in bits_below(heads)[1:]:
            total = total.reshape((total.shape[0] // 2, 2) + total.shape[1:])
            total = total[:, 0] + swap(total[:, 1], "hid", bit)
        shares.append(total[0])
    x_share = swap(shares[0], "tok", 1)
    share = shares[1] + x_share
    from_pair = swap(share[1], "tok", pair)
    input_grad = share[0] + from_pair

    last_total = fold(*made[2])
    hand_over(second_total, [shares[0]])
    hand_over(last_total, [x_share])

    quarters = [jnp.concatenate(pieces_of, axis=1) for pieces_of in rows_of]
    for bit in (1, 2):
        flip = mine & bit > 0
        quarters = [jnp.where(flip, quarters[j ^ bit], quarters[j]) for j in range(4)]
    ordered = jnp.concatenate(quarters, axis=1)[:, :blocks]
    return (
        input_grad,
        0.9 * mom_up + scale * ordered[0],
        0.9 * mom_down + scale * ordered[1],
    )


def solution(mesh):
    return jax.shard_map(
        shards,
        mesh=mesh,
        in_specs=(
            P("tok", None),
            P("tok", None),
            P("hid", None, "tok", None),
            P("hid", None, "tok", None),
            P("hid", None),
            P("hid", None),
            P("hid", None, "tok", None),
            P("hid", None, "tok", None),
        ),
        out_specs=(P("tok", "hid"), P("hid", None, "tok", None), P("hid", None, "tok", None)),
        check_vma=False,
    )
```

```python
import functools

import jax
import jax.numpy as jnp
from jax import lax
from jax.experimental import pallas as pl
from jax.experimental.pallas import tpu as pltpu
from jax.sharding import PartitionSpec as P

F32, BF16 = jnp.float32, jnp.bfloat16
NN = (((1,), (0,)), ((), ()))
NT = (((1,), (1,)), ((), ()))


def swap(value, axis, bit):
    size = lax.axis_size(axis)
    return lax.ppermute(value, axis, [(i, i ^ bit) for i in range(size)])


def bits_below(size):
    return [1 << i for i in range(size.bit_length() - 1)]


def inner_size(size):
    inner = 1
    while inner * inner * 8 <= size:
        inner *= 2
    return inner


def split(value):
    high = value.astype(BF16)
    return high, (value - high.astype(F32)).astype(BF16)


def dot(a, b, dims):
    return lax.dot_general(a, b, dims, preferred_element_type=F32)


def kernel(cfg, up_at, down_at, place, *refs):
    starts, sizes, kb, blk, rows, nb, n, q, heads, first, last, awaits = cfg
    fc = sum(sizes)
    refs = list(refs)
    groups = min(n, 2)
    x_own, c_own = refs[:2]
    got, refs = refs[2:2 + 3 * heads], refs[2 + 3 * heads:]
    slabs, refs = refs[:n], refs[n:]
    prev = None
    if not first:
        prev, refs = refs[0], refs[1:]
    refs = refs[awaits:]
    grads = []
    for _ in sizes:
        grads.append(refs[:groups])
        refs = refs[groups:]
    outs, refs = refs[:4 if last else 1], refs[4 if last else 1:]
    w, xb, cb, acc, w_sem, g_sem, x_sem, i_sem = refs
    me, hid = place[0], place[1]
    span = nb // heads

    def weight_copy(r):
        start = pl.multiple_of((me ^ r) * q, q) if n > 1 else 0
        return pltpu.make_async_copy(
            slabs[r].at[:, pl.ds(starts[r], fc)], w.at[:, :, :, pl.ds(start, q), :], w_sem.at[r])

    def grad_copies(act):
        for r in range(n):
            start = pl.multiple_of((me ^ r) * q, q) if n > 1 else 0
            f0 = 0
            for p, size in enumerate(sizes):
                act(pltpu.make_async_copy(
                    w.at[:, pl.ds(f0, size), :, pl.ds(start, q), :],
                    grads[p][r * groups // n].at[r % (n // groups)], g_sem.at[p, r]))
                f0 += size

    def token_copies(f, slot, act):
        for k in range(kb):
            for i, (own, ats, buf) in enumerate(((x_own, up_at, xb), (c_own, down_at, cb))):
                at = ats[f * kb + k]
                col = pl.multiple_of(at * blk, blk)
                act(pltpu.make_async_copy(
                    own.at[:, pl.ds(col, blk)], buf.at[slot, k, pl.ds(0, rows)],
                    x_sem.at[slot, i, k, 0]))
                col = pl.multiple_of(lax.rem(at, span) * blk, blk)
                holder = lax.div(at, span) ^ hid
                for r in range(heads):
                    @pl.when(holder == r)
                    def _():
                        for group in range(1, 4):
                            act(pltpu.make_async_copy(
                                got[(group - 1) * heads + r].at[i, :, pl.ds(col, blk)],
                                buf.at[slot, k, pl.ds(group * rows, rows)],
                                x_sem.at[slot, i, k, group]))

    def start(copy):
        copy.start()

    def wait(copy):
        copy.wait()

    for r in range(n):
        weight_copy(r).start()
    token_copies(0, 0, start)
    if first:
        acc[...] = jnp.zeros_like(acc)
    else:
        fill = pltpu.make_async_copy(prev, acc, i_sem.at[0])
        fill.start()
        fill.wait()
    for r in range(n):
        weight_copy(r).wait()

    def step(f, carry):
        slot = lax.rem(f, 2)

        @pl.when(f + 1 < fc)
        def _():
            token_copies(f + 1, 1 - slot, start)

        token_copies(f, slot, wait)
        xh, xl = split(jnp.concatenate([xb[slot, k] for k in range(kb)], axis=1))
        ch, cl = split(jnp.concatenate([cb[slot, k] for k in range(kb)], axis=1))
        uh, ul = split(w[0, f].reshape(kb * blk, blk))
        dh, dl = split(jnp.concatenate([w[1, f, k] for k in range(kb)], axis=1))

        wide = dot(xh, jnp.concatenate([uh, ul], axis=1), NN)
        pre = wide[:, :blk] + (wide[:, blk:] + dot(xl, uh, NN))
        wide = dot(ch, jnp.concatenate([dh, dl], axis=0), NT)
        grad_act = wide[:, :blk] + (wide[:, blk:] + dot(cl, dh, NT))
        sig = jax.nn.sigmoid(pre)
        act = pre * sig
        grad_pre = grad_act * sig * (1.0 + pre * (1.0 - sig))

        ah, al = split(act.T)
        tall = dot(jnp.concatenate([ah, al], axis=0), ch, NN)
        grad_down = tall[:blk] + (tall[blk:] + dot(ah, cl, NN))
        gh, gl = split(grad_pre.T)
        tall = dot(jnp.concatenate([gh, gl], axis=0), xh, NN)
        grad_up = tall[:blk] + (tall[blk:] + dot(gh, xl, NN))
        ph, plow = split(grad_pre)
        back = dot(jnp.concatenate([ph, plow], axis=1), jnp.concatenate([uh, uh], axis=1), NT)
        back = back + dot(ph, ul, NT)
        for k in range(kb):
            part = slice(k * blk, (k + 1) * blk)
            w[0, f, k] = grad_up[:, part].T
            w[1, f, k] = grad_down[:, part]
            at = up_at[f * kb + k]
            acc[at] = acc[at] + back[:, part]
        return carry

    lax.fori_loop(0, fc, step, 0)
    grad_copies(start)
    if last:
        copies = []
        for r in range(heads):
            for j in range(span):
                for group in range(4):
                    copies.append(pltpu.make_async_copy(
                        acc.at[(hid ^ r) * span + j, pl.ds(group * rows, rows)],
                        outs[2 * (group % 2) + r % 2].at[
                            r // 2, group // 2, :, pl.ds(j * blk, blk)],
                        i_sem.at[len(copies)]))
    else:
        copies = [pltpu.make_async_copy(acc, outs[0], i_sem.at[0])]
    for copy in copies:
        copy.start()
    for copy in copies:
        copy.wait()
    grad_copies(wait)


def block_pass(x, cot, got, slabs, up_at, down_at, me, hid, tok, heads, prev, sizes, last, awaits, loose):
    fc = up_at.shape[0]
    n = len(slabs)
    starts, parts = zip(*slabs)
    kb, q, blk = parts[0].shape[2:]
    rows, width = x.shape
    nb = width // blk
    first = prev is None
    cfg = (starts, sizes, kb, blk, rows, nb, n, q, heads, first, last, len(awaits))
    groups = min(n, 2)
    out = [jax.ShapeDtypeStruct((n // groups, 2, size, kb, q, blk), F32)
           for size in sizes for _ in range(groups)]
    if last:
        out += [jax.ShapeDtypeStruct((heads // 2, 2, rows, width // heads), F32)] * 4
    else:
        out.append(pltpu.HBM((nb, 4 * rows, blk), F32))
    def fixed(*arrays):
        return [pltpu.with_memory_space_constraint(a, pltpu.HBM) for a in arrays]

    parts = [part if loose[r] else fixed(part)[0] for r, part in enumerate(parts)]
    late = {2 * heads - 1, 3 * heads - 2, 3 * heads - 1}
    got = [a if r in late else fixed(a)[0] for r, a in enumerate(got)]
    operands = fixed(x, cot) + got + parts + ([] if first else fixed(prev)) + awaits
    anywhere = pl.BlockSpec(memory_space=pl.ANY)
    products = 4 * rows * fc * kb * blk * blk
    results = pl.pallas_call(
        functools.partial(kernel, cfg),
        out_shape=out,
        grid_spec=pltpu.PrefetchScalarGridSpec(
            num_scalar_prefetch=3,
            grid=(1,),
            in_specs=[anywhere] * len(operands),
            out_specs=[anywhere] * len(out),
            scratch_shapes=[
                pltpu.VMEM((2, fc, kb, blk, blk), F32),
                pltpu.VMEM((2, kb, 4 * rows, blk), F32),
                pltpu.VMEM((2, kb, 4 * rows, blk), F32),
                pltpu.VMEM((nb, 4 * rows, blk), F32),
                pltpu.SemaphoreType.DMA((n,)),
                pltpu.SemaphoreType.DMA((len(sizes), n)),
                pltpu.SemaphoreType.DMA((2, 2, kb, 4)),
                pltpu.SemaphoreType.DMA((4 * nb,)),
            ],
        ),
        compiler_params=pltpu.CompilerParams(vmem_limit_bytes=24 * 2**20),
        cost_estimate=pl.CostEstimate(
            flops=8 * 5 * 3 * products, bytes_accessed=16 * 2**20, transcendentals=0),
    )(up_at.reshape(-1), down_at.reshape(-1), jnp.stack([me, hid]), *operands)
    grads = []
    for p, size in enumerate(sizes):
        pair = results[p * groups:(p + 1) * groups]
        if n == 1:
            whole = pair[0].reshape(2, size, kb, tok, q // tok, blk)
            whole = jnp.take(jnp.moveaxis(whole, 3, 0), me ^ jnp.arange(tok), axis=0)
            whole = whole.reshape((2, tok // 2) + whole.shape[1:])
            pair = whole[0], whole[1]
        grads.append(pair)
    return grads, results[len(sizes) * groups:]


def after(value, *others):
    return lax.optimization_barrier((value, *others))[0]


def shards(inputs, cotangent, up_blocks, down_blocks, up_index, down_index, mom_up, mom_down):
    rows, width = inputs.shape
    blocks, kb, q, blk = up_blocks.shape
    tok, heads = lax.axis_size("tok"), lax.axis_size("hid")
    me, hid = lax.axis_index("tok"), lax.axis_index("hid")
    pair = inner_size(tok)
    most = [b for b in bits_below(tok) if b not in (1, pair)]
    quarter = -(-blocks // 4)
    if quarter * 4 != blocks:
        extra = 4 * quarter - blocks
        up_blocks, down_blocks = (
            jnp.pad(a, ((0, extra), (0, 0), (0, 0), (0, 0))) for a in (up_blocks, down_blocks))
        up_index, down_index = (jnp.pad(a, ((0, extra), (0, 0))) for a in (up_index, down_index))
    cuts = [round(quarter * part / 7) for part in (0, 2, 5, 7)]
    calls = [cuts[:2], cuts[1:]]
    mine = (me // pair) % 2 * 2 + me % 2
    scale = (rows * tok) ** (-0.5)
    span = width // heads

    def weights(which):
        at = which * quarter
        return [lax.dynamic_slice(a, (at, 0, 0, 0), (quarter, kb, q, blk))
                for a in (up_blocks, down_blocks)]

    both = jnp.stack([
        lax.dynamic_slice(a, (0, hid * span), (rows, span)) for a in (inputs, cotangent)])
    x_tokens = swap(both, "tok", 1)
    z_tokens = swap(both, "tok", pair)

    keep = {0: jnp.stack(weights(mine)), pair: jnp.stack(weights(mine ^ 2))}
    give = jnp.stack([jnp.stack(weights(mine ^ 1)), jnp.stack(weights(mine ^ 3))])
    masks = [sum(b for i, b in enumerate(most) if j >> i & 1) for j in range(2 ** len(most))]
    far = [m | p for m in reversed(masks) if m for p in (pair, 0)]

    parts = {0: keep[0]}
    waits = []
    for to in far:
        parts[to] = swap(after(keep[to & pair], *waits), "tok", to)
        waits = [parts[to]]
    given = swap(after(give, x_tokens), "tok", 1)
    parts[1] = given[0]
    second = {0: given[0], pair: given[1]}
    parts[pair] = swap(after(keep[pair], z_tokens), "tok", pair)
    for to in far:
        parts[to | 1] = swap(after(second[to & pair], *waits), "tok", to)
        waits = [parts[to | 1]]
    parts[pair | 1] = swap(after(second[pair], parts[pair]), "tok", pair)

    xz_tokens = swap(after(z_tokens, given), "tok", 1)
    order = [
        (x_tokens, [parts[far[0]]]),
        (z_tokens, [parts[far[-1]]]),
        (xz_tokens, [parts[far[0] | 1], parts[pair]]),
    ]
    got = []
    crossed_y = []
    for fetched, held in order:
        pieces = {0: after(fetched, *held, *crossed_y)}
        for bit in reversed(bits_below(heads)[1:]):
            for r in list(pieces):
                pieces[r | bit] = swap(pieces[r], "hid", bit)
        crossed_y = [pieces[heads - 2]]
        for r in list(pieces):
            pieces[r | 1] = swap(pieces[r], "hid", 1)
        got.append([pieces[r] for r in range(heads)])
    got = got[0] + got[1] + got[2]

    slabs_of = [parts[r] for r in range(tok)]
    partial, made = None, []
    for call in calls:
        f0, f1 = call[0], call[-1]
        slabs = [(f0, part) for part in slabs_of]
        if q % 8:
            whole = jnp.stack([part[:, f0:f1] for part in slabs_of])
            whole = jnp.take(whole, me ^ jnp.arange(tok), axis=0)
            slabs = [(0, jnp.moveaxis(whole, 0, 3).reshape(2, f1 - f0, kb, blk, blk))]
        at = (mine * quarter + f0, 0)
        grads, rest = block_pass(
            inputs, cotangent, got, slabs,
            lax.dynamic_slice(up_index, at, (f1 - f0, kb)),
            lax.dynamic_slice(down_index, at, (f1 - f0, kb)),
            me, hid, tok, heads, partial,
            [b - a for a, b in zip(call[:-1], call[1:])], f1 == quarter, [], [False] * tok)
        partial = rest[0]

        made += grads

    rows_of = [[] for _ in range(4)]
    folded, sent = [], []

    def fold(low, high, *others):
        back = swap(after(high, *folded[-1:], *others), "tok", tok // 2)
        folded.append(back)
        total = low + back
        left = list(reversed(bits_below(tok)))[1:]
        for bit in reversed(most[:-1]):
            p = left.index(bit)
            left.remove(bit)
            total = total.reshape((2 ** p, 2, -1) + total.shape[1:])
            total = (total[:, 0] + swap(total[:, 1], "tok", bit)).reshape((-1,) + total.shape[3:])
        return total

    def hand_over(total, x_waits=(), z_waits=()):
        crossed = swap(after(total[1::2], *sent[-1:], *x_waits), "tok", 1)
        over = swap(after(jnp.stack([total[2], crossed[1]]), *z_waits), "tok", pair)
        sent.append(over)
        for r, got_rows in enumerate((total[0], crossed[0], over[0], over[1])):
            rows_of[r].append(got_rows)

    hand_over(fold(*made[0]))
    second_total = fold(*made[1])

    shares = []
    for x_side in (1, 0):
        even, odd = rest[2 * x_side:2 * x_side + 2]
        total = even + swap(after(odd, folded[0]), "hid", 1)
        for bit in bits_below(heads)[1:]:
            total = total.reshape((total.shape[0] // 2, 2) + total.shape[1:])
            total = total[:, 0] + swap(total[:, 1], "hid", bit)
        shares.append(total[0])
    x_share = swap(shares[0], "tok", 1)
    share = shares[1] + x_share
    from_pair = swap(share[1], "tok", pair)
    input_grad = share[0] + from_pair

    last_total = fold(*made[2])
    hand_over(second_total, [shares[0]])
    hand_over(last_total, [x_share], [from_pair])

    quarters = [jnp.concatenate(pieces_of, axis=1) for pieces_of in rows_of]
    for bit in (1, 2):
        flip = mine & bit > 0
        quarters = [jnp.where(flip, quarters[j ^ bit], quarters[j]) for j in range(4)]
    ordered = jnp.concatenate(quarters, axis=1)[:, :blocks]
    return (
        input_grad,
        0.9 * mom_up + scale * ordered[0],
        0.9 * mom_down + scale * ordered[1],
    )


def solution(mesh):
    return jax.shard_map(
        shards,
        mesh=mesh,
        in_specs=(
            P("tok", None),
            P("tok", None),
            P("hid", None, "tok", None),
            P("hid", None, "tok", None),
            P("hid", None),
            P("hid", None),
            P("hid", None, "tok", None),
            P("hid", None, "tok", None),
        ),
        out_specs=(P("tok", "hid"), P("hid", None, "tok", None), P("hid", None, "tok", None)),
        check_vma=False,
    )
```

```python
import functools

import jax
import jax.numpy as jnp
from jax import lax
from jax.experimental import pallas as pl
from jax.experimental.pallas import tpu as pltpu
from jax.sharding import PartitionSpec as P

F32, BF16 = jnp.float32, jnp.bfloat16
NN = (((1,), (0,)), ((), ()))
NT = (((1,), (1,)), ((), ()))


def swap(value, axis, bit):
    size = lax.axis_size(axis)
    return lax.ppermute(value, axis, [(i, i ^ bit) for i in range(size)])


def bits_below(size):
    return [1 << i for i in range(size.bit_length() - 1)]


def inner_size(size):
    inner = 1
    while inner * inner * 8 <= size:
        inner *= 2
    return inner


def split(value):
    high = value.astype(BF16)
    return high, (value - high.astype(F32)).astype(BF16)


def dot(a, b, dims):
    return lax.dot_general(a, b, dims, preferred_element_type=F32)


def kernel(cfg, up_at, down_at, place, *refs):
    starts, sizes, kb, blk, rows, nb, n, q, heads, first, last, awaits = cfg
    fc = sum(sizes)
    refs = list(refs)
    groups = min(n, 2)
    x_own, c_own = refs[:2]
    got, refs = refs[2:2 + 3 * heads], refs[2 + 3 * heads:]
    slabs, refs = refs[:n], refs[n:]
    prev = None
    if not first:
        prev, refs = refs[0], refs[1:]
    refs = refs[awaits:]
    grads = []
    for _ in sizes:
        grads.append(refs[:groups])
        refs = refs[groups:]
    outs, refs = refs[:4 if last else 1], refs[4 if last else 1:]
    w, xb, cb, acc, w_sem, g_sem, x_sem, i_sem = refs
    me, hid = place[0], place[1]
    span = nb // heads

    def weight_copy(r):
        start = pl.multiple_of((me ^ r) * q, q) if n > 1 else 0
        return pltpu.make_async_copy(
            slabs[r].at[:, pl.ds(starts[r], fc)], w.at[:, :, :, pl.ds(start, q), :], w_sem.at[r])

    def grad_copies(act):
        for r in range(n):
            start = pl.multiple_of((me ^ r) * q, q) if n > 1 else 0
            f0 = 0
            for p, size in enumerate(sizes):
                act(pltpu.make_async_copy(
                    w.at[:, pl.ds(f0, size), :, pl.ds(start, q), :],
                    grads[p][r * groups // n].at[r % (n // groups)], g_sem.at[p, r]))
                f0 += size

    def token_copies(f, slot, act):
        for k in range(kb):
            for i, (own, ats, buf) in enumerate(((x_own, up_at, xb), (c_own, down_at, cb))):
                at = ats[f * kb + k]
                col = pl.multiple_of(at * blk, blk)
                act(pltpu.make_async_copy(
                    own.at[:, pl.ds(col, blk)], buf.at[slot, k, pl.ds(0, rows)],
                    x_sem.at[slot, i, k, 0]))
                col = pl.multiple_of(lax.rem(at, span) * blk, blk)
                holder = lax.div(at, span) ^ hid
                for r in range(heads):
                    @pl.when(holder == r)
                    def _():
                        for group in range(1, 4):
                            act(pltpu.make_async_copy(
                                got[(group - 1) * heads + r].at[i, :, pl.ds(col, blk)],
                                buf.at[slot, k, pl.ds(group * rows, rows)],
                                x_sem.at[slot, i, k, group]))

    def start(copy):
        copy.start()

    def wait(copy):
        copy.wait()

    for r in range(n):
        weight_copy(r).start()
    token_copies(0, 0, start)
    if first:
        acc[...] = jnp.zeros_like(acc)
    else:
        fill = pltpu.make_async_copy(prev, acc, i_sem.at[0])
        fill.start()
        fill.wait()
    for r in range(n):
        weight_copy(r).wait()

    def step(f, carry):
        slot = lax.rem(f, 2)

        @pl.when(f + 1 < fc)
        def _():
            token_copies(f + 1, 1 - slot, start)

        token_copies(f, slot, wait)
        xh, xl = split(jnp.concatenate([xb[slot, k] for k in range(kb)], axis=1))
        ch, cl = split(jnp.concatenate([cb[slot, k] for k in range(kb)], axis=1))
        uh, ul = split(w[0, f].reshape(kb * blk, blk))
        dh, dl = split(jnp.concatenate([w[1, f, k] for k in range(kb)], axis=1))

        wide = dot(xh, jnp.concatenate([uh, ul], axis=1), NN)
        pre = wide[:, :blk] + (wide[:, blk:] + dot(xl, uh, NN))
        wide = dot(ch, jnp.concatenate([dh, dl], axis=0), NT)
        grad_act = wide[:, :blk] + (wide[:, blk:] + dot(cl, dh, NT))
        sig = jax.nn.sigmoid(pre)
        act = pre * sig
        grad_pre = grad_act * sig * (1.0 + pre * (1.0 - sig))

        ah, al = split(act.T)
        tall = dot(jnp.concatenate([ah, al], axis=0), ch, NN)
        grad_down = tall[:blk] + (tall[blk:] + dot(ah, cl, NN))
        gh, gl = split(grad_pre.T)
        tall = dot(jnp.concatenate([gh, gl], axis=0), xh, NN)
        grad_up = tall[:blk] + (tall[blk:] + dot(gh, xl, NN))
        ph, plow = split(grad_pre)
        back = dot(jnp.concatenate([ph, plow], axis=1), jnp.concatenate([uh, uh], axis=1), NT)
        back = back + dot(ph, ul, NT)
        for k in range(kb):
            part = slice(k * blk, (k + 1) * blk)
            w[0, f, k] = grad_up[:, part].T
            w[1, f, k] = grad_down[:, part]
            at = up_at[f * kb + k]
            acc[at] = acc[at] + back[:, part]
        return carry

    lax.fori_loop(0, fc, step, 0)
    grad_copies(start)
    if last:
        copies = []
        for r in range(heads):
            for j in range(span):
                for group in range(4):
                    copies.append(pltpu.make_async_copy(
                        acc.at[(hid ^ r) * span + j, pl.ds(group * rows, rows)],
                        outs[2 * (group % 2) + r % 2].at[
                            r // 2, group // 2, :, pl.ds(j * blk, blk)],
                        i_sem.at[len(copies)]))
    else:
        copies = [pltpu.make_async_copy(acc, outs[0], i_sem.at[0])]
    for copy in copies:
        copy.start()
    for copy in copies:
        copy.wait()
    grad_copies(wait)


def block_pass(x, cot, got, slabs, up_at, down_at, me, hid, tok, heads, prev, sizes, last, awaits, loose):
    fc = up_at.shape[0]
    n = len(slabs)
    starts, parts = zip(*slabs)
    kb, q, blk = parts[0].shape[2:]
    rows, width = x.shape
    nb = width // blk
    first = prev is None
    cfg = (starts, sizes, kb, blk, rows, nb, n, q, heads, first, last, len(awaits))
    groups = min(n, 2)
    out = [jax.ShapeDtypeStruct((n // groups, 2, size, kb, q, blk), F32)
           for size in sizes for _ in range(groups)]
    if last:
        out += [jax.ShapeDtypeStruct((heads // 2, 2, rows, width // heads), F32)] * 4
    else:
        out.append(pltpu.HBM((nb, 4 * rows, blk), F32))
    def fixed(*arrays):
        return [pltpu.with_memory_space_constraint(a, pltpu.HBM) for a in arrays]

    parts = [part if loose[r] else fixed(part)[0] for r, part in enumerate(parts)]
    late = {2 * heads - 1, 3 * heads - 2, 3 * heads - 1}
    got = [a if r in late else fixed(a)[0] for r, a in enumerate(got)]
    operands = fixed(x, cot) + got + parts + ([] if first else fixed(prev)) + awaits
    anywhere = pl.BlockSpec(memory_space=pl.ANY)
    products = 4 * rows * fc * kb * blk * blk
    results = pl.pallas_call(
        functools.partial(kernel, cfg),
        out_shape=out,
        grid_spec=pltpu.PrefetchScalarGridSpec(
            num_scalar_prefetch=3,
            grid=(1,),
            in_specs=[anywhere] * len(operands),
            out_specs=[anywhere] * len(out),
            scratch_shapes=[
                pltpu.VMEM((2, fc, kb, blk, blk), F32),
                pltpu.VMEM((2, kb, 4 * rows, blk), F32),
                pltpu.VMEM((2, kb, 4 * rows, blk), F32),
                pltpu.VMEM((nb, 4 * rows, blk), F32),
                pltpu.SemaphoreType.DMA((n,)),
                pltpu.SemaphoreType.DMA((len(sizes), n)),
                pltpu.SemaphoreType.DMA((2, 2, kb, 4)),
                pltpu.SemaphoreType.DMA((4 * nb,)),
            ],
        ),
        compiler_params=pltpu.CompilerParams(vmem_limit_bytes=24 * 2**20),
        cost_estimate=pl.CostEstimate(
            flops=8 * 5 * 3 * products, bytes_accessed=16 * 2**20, transcendentals=0),
    )(up_at.reshape(-1), down_at.reshape(-1), jnp.stack([me, hid]), *operands)
    grads = []
    for p, size in enumerate(sizes):
        pair = results[p * groups:(p + 1) * groups]
        if n == 1:
            whole = pair[0].reshape(2, size, kb, tok, q // tok, blk)
            whole = jnp.take(jnp.moveaxis(whole, 3, 0), me ^ jnp.arange(tok), axis=0)
            whole = whole.reshape((2, tok // 2) + whole.shape[1:])
            pair = whole[0], whole[1]
        grads.append(pair)
    return grads, results[len(sizes) * groups:]


def after(value, *others):
    return lax.optimization_barrier((value, *others))[0]


def shards(inputs, cotangent, up_blocks, down_blocks, up_index, down_index, mom_up, mom_down):
    rows, width = inputs.shape
    blocks, kb, q, blk = up_blocks.shape
    tok, heads = lax.axis_size("tok"), lax.axis_size("hid")
    me, hid = lax.axis_index("tok"), lax.axis_index("hid")
    pair = inner_size(tok)
    most = [b for b in bits_below(tok) if b not in (1, pair)]
    quarter = -(-blocks // 4)
    if quarter * 4 != blocks:
        extra = 4 * quarter - blocks
        up_blocks, down_blocks = (
            jnp.pad(a, ((0, extra), (0, 0), (0, 0), (0, 0))) for a in (up_blocks, down_blocks))
        up_index, down_index = (jnp.pad(a, ((0, extra), (0, 0))) for a in (up_index, down_index))
    cuts = [round(quarter * part / 7) for part in (0, 2, 5, 7)]
    calls = [cuts[:2], cuts[1:]]
    mine = (me // pair) % 2 * 2 + me % 2
    scale = (rows * tok) ** (-0.5)
    span = width // heads

    def weights(which):
        at = which * quarter
        return [lax.dynamic_slice(a, (at, 0, 0, 0), (quarter, kb, q, blk))
                for a in (up_blocks, down_blocks)]

    both = jnp.stack([
        lax.dynamic_slice(a, (0, hid * span), (rows, span)) for a in (inputs, cotangent)])
    x_tokens = swap(both, "tok", 1)
    z_tokens = swap(both, "tok", pair)

    keep = {0: jnp.stack(weights(mine)), pair: jnp.stack(weights(mine ^ 2))}
    give = jnp.stack([jnp.stack(weights(mine ^ 1)), jnp.stack(weights(mine ^ 3))])
    masks = [sum(b for i, b in enumerate(most) if j >> i & 1) for j in range(2 ** len(most))]
    far = [m | p for m in reversed(masks) if m for p in (pair, 0)]

    parts = {0: keep[0]}
    waits = []
    for to in far:
        parts[to] = swap(after(keep[to & pair], *waits), "tok", to)
        waits = [parts[to]]
    given = swap(after(give, x_tokens), "tok", 1)
    parts[1] = given[0]
    second = {0: given[0], pair: given[1]}
    parts[pair] = swap(after(keep[pair], z_tokens), "tok", pair)
    for to in far:
        parts[to | 1] = swap(after(second[to & pair], *waits), "tok", to)
        waits = [parts[to | 1]]
    parts[pair | 1] = swap(after(second[pair], parts[pair]), "tok", pair)

    xz_tokens = swap(after(z_tokens, given), "tok", 1)
    order = [
        (x_tokens, [parts[far[0]]]),
        (z_tokens, [parts[far[-1]]]),
        (xz_tokens, [parts[far[0] | 1], parts[pair]]),
    ]
    got = []
    crossed_y = []
    for fetched, held in order:
        pieces = {0: after(fetched, *held, *crossed_y)}
        for bit in reversed(bits_below(heads)[1:]):
            for r in list(pieces):
                pieces[r | bit] = swap(pieces[r], "hid", bit)
        crossed_y = [pieces[heads - 2]]
        for r in list(pieces):
            pieces[r | 1] = swap(pieces[r], "hid", 1)
        got.append([pieces[r] for r in range(heads)])
    got = got[0] + got[1] + got[2]

    slabs_of = [parts[r] for r in range(tok)]
    total_of, delivered = [], []
    partial, folded = None, []
    for call in calls:
        f0, f1 = call[0], call[-1]
        slabs = [(f0, part) for part in slabs_of]
        if q % 8:
            whole = jnp.stack([part[:, f0:f1] for part in slabs_of])
            whole = jnp.take(whole, me ^ jnp.arange(tok), axis=0)
            slabs = [(0, jnp.moveaxis(whole, 0, 3).reshape(2, f1 - f0, kb, blk, blk))]
        at = (mine * quarter + f0, 0)
        grads, rest = block_pass(
            inputs, cotangent, got, slabs,
            lax.dynamic_slice(up_index, at, (f1 - f0, kb)),
            lax.dynamic_slice(down_index, at, (f1 - f0, kb)),
            me, hid, tok, heads, partial,
            [b - a for a, b in zip(call[:-1], call[1:])], f1 == quarter, [], [False] * tok)
        partial = rest[0]

        for low, high in grads:
            back = swap(after(high, *folded[-1:], *delivered[-1:]), "tok", tok // 2)
            folded.append(back)
            total = low + back
            left = list(reversed(bits_below(tok)))[1:]
            for bit in reversed(most[:-1]):
                p = left.index(bit)
                left.remove(bit)
                total = total.reshape((2 ** p, 2, -1) + total.shape[1:])
                total = (total[:, 0] + swap(total[:, 1], "tok", bit)).reshape(
                    (-1,) + total.shape[3:])
            total_of.append(total)

    rows_of = [[] for _ in range(4)]
    for total in total_of[:-1]:
        crossed = swap(total[1::2], "tok", 1)
        over = swap(jnp.stack([total[2], crossed[1]]), "tok", pair)
        for r, got_rows in enumerate((total[0], crossed[0], over[0], over[1])):
            rows_of[r].append(got_rows)
    shares, firsts = [], folded[:1]
    for x_side in (1, 0):
        even, odd = rest[2 * x_side:2 * x_side + 2]
        first = swap(after(odd, *firsts), "hid", 1)
        total = even + first
        for bit in bits_below(heads)[1:]:
            total = total.reshape((total.shape[0] // 2, 2) + total.shape[1:])
            total = total[:, 0] + swap(total[:, 1], "hid", bit)
        shares.append(total[0])
    share = shares[1] + swap(shares[0], "tok", 1)
    from_pair = swap(share[1], "tok", pair)
    input_grad = share[0] + from_pair

    for r, to in enumerate((0, 1, pair, pair | 1)):
        rows_of[r].append(swap(after(total_of[-1][r], *([from_pair] if to & pair else [])), "tok", to) if to else total_of[-1][0])

    quarters = [jnp.concatenate(pieces_of, axis=1) for pieces_of in rows_of]
    for bit in (1, 2):
        flip = mine & bit > 0
        quarters = [jnp.where(flip, quarters[j ^ bit], quarters[j]) for j in range(4)]
    ordered = jnp.concatenate(quarters, axis=1)[:, :blocks]
    return (
        input_grad,
        0.9 * mom_up + scale * ordered[0],
        0.9 * mom_down + scale * ordered[1],
    )


def solution(mesh):
    return jax.shard_map(
        shards,
        mesh=mesh,
        in_specs=(
            P("tok", None),
            P("tok", None),
            P("hid", None, "tok", None),
            P("hid", None, "tok", None),
            P("hid", None),
            P("hid", None),
            P("hid", None, "tok", None),
            P("hid", None, "tok", None),
        ),
        out_specs=(P("tok", "hid"), P("hid", None, "tok", None), P("hid", None, "tok", None)),
        check_vma=False,
    )
```
